32 devices in a mesh: rot: 4 (over y, core), tile: 4 (over z), nar: 2 (over x).
Axes of the slice: x: 2, y: 2, z: 4, core: 2. Of those that a mesh axis runs over, the one named last changes fastest.
Arguments:
- interp_index: int32 [8, 8, 2, 192, 384], P(None, 'rot', 'nar', 'tile'), may hold values from 0 to 4095
- interp_weight: bfloat16 [8, 8, 2, 192, 384], P(None, 'rot', 'nar', 'tile'), may hold values from 0 to 0.25
- volume: bfloat16 [2, 2, 4, 4096], P(None, 'nar', 'tile'), may hold values from -6 to 6
- spectrum: bfloat16 [2, 4, 2, 192, 384], P(None, 'tile', 'nar'), may hold values from -6 to 6
- ctf_filter: bfloat16 [4, 2, 192, 384], P('tile', 'nar'), may hold values from -1 to 1
- peak_count: int32 [4, 4], P('rot', 'tile'), may hold values from 1 to 4, 9 in all within a row
- peak_orient: int32 [64], P(('rot', 'tile')), may hold values from 0 to 1
- peak_row: int32 [64], P(('rot', 'tile')), may hold values from 0 to 383
- peak_col: int32 [64], P(('rot', 'tile')), may hold values from 0 to 383
- ctf_grid: bfloat16 [32, 2, 18432], P('tile', 'nar'), may hold values from -1 to 1
Outputs:
- peak_max: float32 [4, 2, 73728], P('tile', 'nar')
- peak_mean: float32 [4, 2, 73728], P('tile', 'nar')
- refined: float32 [4, 16, 32], P('rot', None, 'tile')
- best: float32 [4, 16], P('rot')
The draws below stay inside these ranges and needn't reach their ends.
Inputs may be any that keep to these rules, and one draw needn't show every extreme that they name: `peak_count`: in each orientation group the counts over all tiles sum to 9, and some tile has exactly 4.
All inputs are finite; a program needn't handle non-finite values.
Results may differ from the reference program's by a relative error of at most 0.013.
Values may be sent and summed in bfloat16 or wider, within the bound.
A program may use at most 128 MiB of HBM per device.

```python
import math
import jax
import jax.numpy as jnp
import numpy as np
from jax import lax

TL = 384
K = 8
VOX = 4096
ORI = 2
MOST = 4
HALF = 192
SROWS = 48
BINS = 18432
ORIENTS = 8
PTOTAL = 9
PEAKS = 64
DEFOCI = 32
N_ROT = 4
N_TILE = 4
N_NAR = 2


def set_ends(entries, stream_key, low, largest):
    place = [jax.random.randint(jax.random.fold_in(stream_key, axis), (), 0, length) for axis, length in enumerate(entries.shape)]
    main_axis = entries.shape.index(max(entries.shape))
    next_to = place[:main_axis] + [(place[main_axis] + 1) % entries.shape[main_axis]] + place[main_axis + 1:]
    return entries.at[tuple(place)].set(low).at[tuple(next_to)].set(largest)


def levels(own_key, extent, pieces, low, largest):
    gain, own = 1.0, jax.random.fold_in(own_key, 6)
    for position, blocks in pieces:
        steps = jnp.exp(jax.random.uniform(jax.random.fold_in(own, position), (blocks,), jnp.float32, low / len(pieces), largest / len(pieces)))
        gain = gain * jnp.repeat(steps, extent[position] // blocks).reshape([-1 if axis == position else 1 for axis in range(len(extent))])
    return gain


def length_profile(amount, total, bound, lean):
    weights = [(1 << 20) // math.isqrt(rank ** lean) + 1 for rank in range(2, amount + 1)]
    rest, counts = total - bound - (amount - 1), [1] * (amount - 1)
    while rest > 0:
        free = [i for i in range(amount - 1) if counts[i] < bound]
        pool, budget = sum([weights[i] for i in free]), rest
        for i in free:
            addition = min(bound - counts[i], max(1, budget * weights[i] // pool), rest)
            counts[i] = counts[i] + addition
            rest = rest - addition
    return np.array([bound] + counts)


def ragged_sizes(key, amount, total, reach, skew):
    if amount == 2:
        one = jax.random.randint(key, (), max(1, total - reach), min(reach, total - 1) + 1)
        return jnp.stack([one, total - one])
    lengths = jnp.asarray(length_profile(amount, total, reach, skew), jnp.int32)
    pairs = (amount - 1) // 2
    source_of, receiver = lengths[1:1 + 2 * pairs:2], lengths[2:2 + 2 * pairs:2]
    margin = jnp.minimum(source_of - 1, reach - receiver)
    passed = jax.random.randint(jax.random.fold_in(key, 1), (pairs,), 0, 1 << 20) % (margin + 1)
    lengths = lengths.at[1:1 + 2 * pairs:2].set(source_of - passed).at[2:2 + 2 * pairs:2].set(receiver + passed)
    return lengths[jax.random.permutation(jax.random.fold_in(key, 2), amount)]


def gaussian(stream_key, extent, width, most, pieces=(), kind=jnp.bfloat16):
    entries = width * jax.random.normal(stream_key, extent, jnp.float32)
    if pieces:
        entries = entries * levels(stream_key, extent, pieces, -0.22, 0.18)
    return jnp.clip(entries, -most, most).astype(kind)


def setup_inputs(seed: int = 0) -> dict:
    key_list = jax.random.split(jax.random.key(seed), 11)
    interp_index = set_ends(jax.random.randint(key_list[0], (K, ORIENTS, N_NAR, HALF, TL), 0, VOX), jax.random.fold_in(key_list[0], 1), 0, VOX - 1).astype(jnp.int32)
    interp_weight = jnp.clip(0.25 * jax.random.uniform(key_list[1], (K, ORIENTS, N_NAR, HALF, TL), jnp.float32) ** levels(key_list[1], (K, ORIENTS, N_NAR, HALF, TL), ((1, 4), (2, 2), (3, 4)), -0.2, 0.2), 0.0, 0.25).astype(jnp.bfloat16)
    volume = gaussian(key_list[2], (2, N_NAR, N_TILE, VOX), 1.0, 6.0, ((1, 2), (2, 4)))
    spectrum = gaussian(key_list[3], (2, N_TILE, N_NAR, HALF, TL), 1.0, 6.0, ((1, 4), (2, 2)))
    ctf_filter = jnp.clip(jax.random.uniform(key_list[4], (N_TILE, N_NAR, HALF, TL), jnp.float32, -1.0, 1.0) * levels(key_list[4], (N_TILE, N_NAR, HALF, TL), ((0, 4), (1, 2)), -0.4, 0.0), -1.0, 1.0).astype(jnp.bfloat16)
    peak_count = jax.vmap(lambda own: ragged_sizes(own, N_TILE, PTOTAL, MOST, 2))(jax.random.split(key_list[5], N_ROT)).reshape((N_ROT, N_TILE)).astype(jnp.int32)
    peak_orient = set_ends(jax.random.randint(key_list[6], (PEAKS,), 0, ORI), jax.random.fold_in(key_list[6], 1), 0, ORI - 1).astype(jnp.int32)
    peak_row = set_ends(jax.random.randint(key_list[7], (PEAKS,), 0, TL), jax.random.fold_in(key_list[7], 1), 0, TL - 1).astype(jnp.int32)
    peak_col = set_ends(jax.random.randint(key_list[8], (PEAKS,), 0, TL), jax.random.fold_in(key_list[8], 1), 0, TL - 1).astype(jnp.int32)
    ctf_grid = jnp.clip(jax.random.uniform(key_list[9], (DEFOCI, N_NAR, BINS), jnp.float32, -1.0, 1.0) * levels(key_list[9], (DEFOCI, N_NAR, BINS), ((0, 4), (1, 2)), -0.4, 0.0), -1.0, 1.0).astype(jnp.bfloat16)
    return dict(interp_index=interp_index, interp_weight=interp_weight, volume=volume, spectrum=spectrum, ctf_filter=ctf_filter, peak_count=peak_count, peak_orient=peak_orient, peak_row=peak_row, peak_col=peak_col, ctf_grid=ctf_grid)


def dft_tables(length):
    steps = jnp.arange(length, dtype=jnp.int32)
    phase = ((steps[:, None] * steps[None, :]) % length).astype(jnp.float32) * (2.0 * jnp.pi / length)
    cosv = jnp.cos(phase).astype(jnp.bfloat16)
    sinv = jnp.sin(phase).astype(jnp.bfloat16)
    wide = jnp.concatenate([jnp.concatenate([cosv, sinv], 1), jnp.concatenate([-sinv, cosv], 1)], 0)
    back = jnp.stack([cosv, -sinv], axis=1)
    return wide, back


def reference(interp_index, interp_weight, volume, spectrum, ctf_filter, peak_count, peak_orient, peak_row, peak_col, ctf_grid):
    vol_rows = jnp.repeat(volume, SROWS, axis=2)
    narrow = jnp.arange(N_NAR, dtype=jnp.int32)[None, :, None, None]
    rowpos = jnp.arange(HALF, dtype=jnp.int32)[None, None, :, None]

    def project(pair):
        index_o, weight_o = pair
        values = vol_rows[:, narrow, rowpos, index_o]
        return jnp.sum(weight_o.astype(jnp.float32)[None] * values.astype(jnp.float32), axis=1).astype(jnp.bfloat16)

    slices = lax.map(project, (jnp.moveaxis(interp_index, 1, 0), jnp.moveaxis(interp_weight, 1, 0)))
    slices = slices.reshape(ORIENTS, 2, TL, TL)
    wide, back = dft_tables(TL)
    back_f = back.astype(jnp.float32)

    def per_tile(t):
        spec = spectrum[:, t].reshape(2, TL, TL).astype(jnp.float32)
        filt = ctf_filter[t].reshape(TL, TL).astype(jnp.float32)
        sr = slices[:, 0].astype(jnp.float32)
        si = slices[:, 1].astype(jnp.float32)
        cr = filt * sr
        ci = filt * si
        xr = spec[0] * cr + spec[1] * ci
        xi = spec[1] * cr - spec[0] * ci
        cross = jnp.stack([xr, xi], axis=2).astype(jnp.bfloat16)
        halfimg = jnp.dot(cross.reshape(ORIENTS * TL, 2 * TL), wide, preferred_element_type=jnp.float32)
        halfimg = halfimg.astype(jnp.bfloat16).reshape(ORIENTS, TL, 2, TL)
        corr = jnp.einsum('yck,okcx->oyx', back_f, halfimg.astype(jnp.float32)) * (1.0 / TL)
        top = jnp.max(corr, axis=0)
        mean = jnp.sum(corr, axis=0) / ORIENTS
        return top, mean

    peak_max, peak_mean = lax.map(per_tile, jnp.arange(N_TILE, dtype=jnp.int32))
    peak_max = peak_max.reshape(N_TILE, TL, N_NAR, HALF).transpose(0, 2, 1, 3).reshape(N_TILE, N_NAR, TL * HALF)
    peak_mean = peak_mean.reshape(N_TILE, TL, N_NAR, HALF).transpose(0, 2, 1, 3).reshape(N_TILE, N_NAR, TL * HALF)

    freq = jnp.arange(TL, dtype=jnp.int32)
    slot = jnp.arange(MOST, dtype=jnp.int32)

    def per_list(index):
        r = index // N_TILE
        t = index % N_TILE
        rows = index * MOST + slot
        orient = (r * ORI + peak_orient[rows]).astype(jnp.int32)
        y0 = peak_row[rows].astype(jnp.int32)
        x0 = peak_col[rows].astype(jnp.int32)
        spec = spectrum[:, t].reshape(2, TL, TL).astype(jnp.float32)
        chosen = slices[orient].astype(jnp.float32)
        pr = (spec[0][None] * chosen[:, 0] + spec[1][None] * chosen[:, 1]).astype(jnp.bfloat16).astype(jnp.float32)
        pi = (spec[1][None] * chosen[:, 0] - spec[0][None] * chosen[:, 1]).astype(jnp.bfloat16).astype(jnp.float32)
        turns = (freq[None, :, None] * y0[:, None, None] + freq[None, None, :] * x0[:, None, None]) % TL
        phase = turns.astype(jnp.float32) * (2.0 * jnp.pi / TL)
        shifted = pr * jnp.cos(phase) - pi * jnp.sin(phase)
        binned = jnp.sum(shifted.reshape(MOST, TL, TL // 4, 4), axis=3).astype(jnp.bfloat16)
        valid = slot < peak_count[r, t]
        binned = jnp.where(valid[:, None, None], binned, jnp.zeros_like(binned))
        return binned.reshape(MOST, N_NAR, BINS)

    binned_all = lax.map(per_list, jnp.arange(N_ROT * N_TILE, dtype=jnp.int32))
    binned_all = binned_all.reshape(N_ROT, N_TILE * MOST, N_NAR, BINS)
    refined = jnp.einsum('rpnb,qnb->rpq', binned_all.astype(jnp.float32), ctf_grid.astype(jnp.float32)) * (1.0 / TL)
    best = jnp.max(refined, axis=2)
    return peak_max, peak_mean, refined, best
```

```python
import functools

import jax
import jax.numpy as jnp
from jax import lax
from jax.experimental import pallas as pl
from jax.experimental.pallas import tpu as pltpu
from jax.sharding import PartitionSpec as P

LANES = 128
SUBL = 8
PACK = 16


def select_tree(items, bits):
    for bit in bits:
        items = [jnp.where(bit, b, a) for a, b in zip(items[::2], items[1::2])]
    return items[0]


def spread_table(table_ref, spread):
    for c in range(table_ref.shape[0]):
        for h in range(table_ref.shape[1]):
            row = table_ref[c, pl.ds(h, 1), :]
            spread[c, h] = jnp.broadcast_to(row, (SUBL, LANES))


def lookup(spread, index):
    rows = spread.shape[1]
    low = index & (LANES - 1)
    high = index >> 7
    bits = [((high >> b) & 1) == 1 for b in range(rows.bit_length() - 1)]
    return [
        select_tree(
            [
                jnp.take_along_axis(spread[c, h], low, axis=1, mode="promise_in_bounds")
                for h in range(rows)
            ],
            bits,
        )
        for c in range(spread.shape[0])
    ]


def interpolate_block(spread, index_ref, weight_ref, o, r, col):
    parts = []
    weights = [
        weight_ref[k, o, pl.ds(r, PACK), pl.ds(col, LANES)].astype(jnp.float32)
        for k in range(index_ref.shape[0])
    ]
    for s in range(0, PACK, SUBL):
        total = None
        for k in range(index_ref.shape[0]):
            found = lookup(spread, index_ref[k, o, pl.ds(r + s, SUBL), pl.ds(col, LANES)])
            w = weights[k][s : s + SUBL]
            terms = [w * v for v in found]
            total = terms if total is None else [a + b for a, b in zip(total, terms)]
        parts.append(total)
    return [jnp.concatenate([p[c] for p in parts], axis=0) for c in range(2)]


def interpolate_kernel(table_ref, index_ref, weight_ref, out_ref, spread):
    spread_table(table_ref, spread)
    _, orients, rows, columns = index_ref.shape
    per_row = columns // LANES
    blocks = rows // PACK * per_row

    def step(i, carry):
        o, rest = i // blocks, i % blocks
        r = pl.multiple_of(rest // per_row * PACK, PACK)
        col = pl.multiple_of(rest % per_row * LANES, LANES)
        found = interpolate_block(spread, index_ref, weight_ref, o, r, col)
        for c in range(2):
            out_ref[c, o, pl.ds(r, PACK), pl.ds(col, LANES)] = found[c].astype(jnp.bfloat16)
        return carry

    lax.fori_loop(0, orients * blocks, step, 0)


def interpolate(interp_index, interp_weight, table):
    _, orients, _, rows, columns = interp_index.shape
    index, weight = interp_index[:, :, 0], interp_weight[:, :, 0]
    short = -rows % PACK
    if short:
        pad = ((0, 0), (0, 0), (0, short), (0, 0))
        index, weight = jnp.pad(index, pad), jnp.pad(weight, pad)
    table = table.astype(jnp.float32).reshape(2, -1, LANES)
    vmem = pl.BlockSpec(memory_space=pltpu.VMEM)
    out = pl.pallas_call(
        interpolate_kernel,
        out_shape=jax.ShapeDtypeStruct((2, orients, rows + short, columns), jnp.bfloat16),
        in_specs=[vmem] * 3,
        out_specs=vmem,
        scratch_shapes=[pltpu.VMEM((2, table.shape[1], SUBL, LANES), jnp.float32)],
        compiler_params=pltpu.CompilerParams(vmem_limit_bytes=32 * 2**20),
        name="interpolate",
    )(table, index, weight)
    return out[:, :, None, :rows]


def merged(x, axis, combine):
    everything = jax.tree.map(
        lambda part, kind: lax.all_gather(part.astype(kind), axis), x, (jnp.bfloat16, jnp.bfloat16)
    )

    def take(k):
        return jax.tree.map(lambda part, own: part[k].astype(own.dtype), everything, x)

    return lax.fori_loop(
        1, lax.axis_size(axis), lambda k, so_far: combine(so_far, take(k)), take(0)
    )


def dft_tables(length):
    steps = jnp.arange(length, dtype=jnp.int32)
    phase = (steps[:, None] * steps[None, :] % length).astype(jnp.float32) * (2.0 * jnp.pi / length)
    cosv = jnp.cos(phase).astype(jnp.bfloat16)
    sinv = jnp.sin(phase).astype(jnp.bfloat16)
    wide = jnp.concatenate([jnp.concatenate([cosv, sinv], 1), jnp.concatenate([-sinv, cosv], 1)], 0)
    back = jnp.stack([cosv, -sinv], axis=1)
    return (wide, back)


def combine_stats(first, second):
    return (jnp.maximum(first[0], second[0]), first[1] + second[1])


def shards(
    interp_index,
    interp_weight,
    volume,
    spectrum,
    ctf_filter,
    peak_count,
    peak_orient,
    peak_row,
    peak_col,
    ctf_grid,
):
    table = volume[:, 0, 0]
    weighted = interpolate(interp_index, interp_weight, table)
    length = spectrum.shape[4]
    half = spectrum.shape[3]
    orients = weighted.shape[1]
    slots = peak_orient.shape[0]
    wide, back = dft_tables(length)
    spec = spectrum[:, 0, 0]
    filt = ctf_filter[0, 0]
    piece = lax.all_gather(weighted, "tile", axis=3, tiled=True)
    count = piece.shape[3]
    spec_rows = spec.astype(jnp.float32)
    filt_rows = filt.astype(jnp.float32)
    sr = piece[0, :, 0].astype(jnp.float32)
    si = piece[1, :, 0].astype(jnp.float32)
    cr = filt_rows * sr
    ci = filt_rows * si
    xr = spec_rows[0] * cr + spec_rows[1] * ci
    xi = spec_rows[1] * cr - spec_rows[0] * ci
    cross = jnp.stack([xr, xi], axis=2).astype(jnp.bfloat16)
    rows_out = jnp.dot(
        cross.reshape(orients * count, 2 * length), wide, preferred_element_type=jnp.float32
    )
    rows_out = rows_out.astype(jnp.bfloat16).reshape(orients, count, 2, length)
    picked_r = jnp.take(sr, peak_orient, axis=0)
    picked_i = jnp.take(si, peak_orient, axis=0)
    plain_r = spec_rows[0] * picked_r + spec_rows[1] * picked_i
    plain_i = spec_rows[1] * picked_r - spec_rows[0] * picked_i
    plain = jnp.stack([plain_r, plain_i], axis=2).astype(jnp.bfloat16)
    combined = jnp.concatenate([rows_out, plain], axis=0)
    halfimg = combined[:orients]
    plain = combined[orients:].astype(jnp.float32)
    offset = lax.axis_index("nar") * half
    back_rows = lax.dynamic_slice_in_dim(back, offset, half, 2)
    partial_value = jnp.einsum(
        "yck,okcx->oyx", back_rows, halfimg, preferred_element_type=jnp.float32
    )
    summed = lax.psum_scatter(
        partial_value.astype(jnp.bfloat16), "nar", scatter_dimension=2, tiled=True
    ).astype(jnp.float32)
    corr = summed * (1.0 / length)
    local_max = jnp.max(corr, axis=0)
    local_sum = jnp.sum(corr, axis=0)
    group_count = lax.axis_size("rot")
    top, total = merged((local_max, local_sum), "rot", combine_stats)
    mean = total / (orients * group_count)
    freq_rows = lax.axis_index("nar") * half + jnp.arange(half, dtype=jnp.int32)
    freq_cols = jnp.arange(length, dtype=jnp.int32)
    unit = 2.0 * jnp.pi / length
    row_turn = ((freq_rows[None, :] * peak_row[:, None]) % length).astype(jnp.float32) * unit
    col_turn = ((freq_cols[None, :] * peak_col[:, None]) % length).astype(jnp.float32) * unit
    rc, rs = jnp.cos(row_turn)[:, :, None], jnp.sin(row_turn)[:, :, None]
    cc, cs = jnp.cos(col_turn)[:, None, :], jnp.sin(col_turn)[:, None, :]
    shifted = plain[:, :, 0] * (rc * cc - rs * cs) - plain[:, :, 1] * (rs * cc + rc * cs)
    binned = jnp.sum(shifted.reshape(slots, half, length // 4, 4), axis=3).astype(jnp.bfloat16)
    valid = jnp.arange(slots, dtype=jnp.int32) < peak_count[0, 0]
    binned = jnp.where(valid[:, None, None], binned, jnp.zeros_like(binned)).reshape(slots, -1)
    grid_local = ctf_grid[:, 0]
    grid_count = grid_local.shape[0]
    listed = lax.axis_size("tile") * slots
    part = lax.dot_general(
        lax.all_gather(binned, "tile", axis=0, tiled=True),
        grid_local,
        (((1,), (1,)), ((), ())),
        preferred_element_type=jnp.float32,
    )
    refined = lax.psum(part, "nar") * (1.0 / length)
    best = lax.pmax(jnp.max(refined, axis=1), "tile")
    return (
        top.reshape(1, 1, -1),
        mean.reshape(1, 1, -1),
        refined.reshape(1, listed, grid_count),
        best.reshape(1, listed),
    )


def solution(mesh):
    return jax.shard_map(
        shards,
        mesh=mesh,
        in_specs=(
            P(None, "rot", "nar", "tile", None),
            P(None, "rot", "nar", "tile", None),
            P(None, "nar", "tile", None),
            P(None, "tile", "nar", None, None),
            P("tile", "nar", None, None),
            P("rot", "tile"),
            P(("rot", "tile")),
            P(("rot", "tile")),
            P(("rot", "tile")),
            P("tile", "nar", None),
        ),
        out_specs=(
            P("tile", "nar", None),
            P("tile", "nar", None),
            P("rot", None, "tile"),
            P("rot", None),
        ),
        check_vma=False,
    )
```

```python
import functools
import math

import jax
import jax.numpy as jnp
import ml_dtypes
import numpy as np
from jax import lax
from jax.experimental import pallas as pl
from jax.experimental.pallas import tpu as pltpu
from jax.sharding import PartitionSpec as P

LANES = 128
SUBL = 8
PACK = 16


def select_tree(items, bits):
    for bit in bits:
        items = [jnp.where(bit, b, a) for a, b in zip(items[::2], items[1::2])]
    return items[0]


def spread_table(table_ref, spread):
    for c in range(table_ref.shape[0]):
        for h in range(table_ref.shape[1]):
            row = table_ref[c, pl.ds(h, 1), :]
            spread[c, h] = jnp.broadcast_to(row, (SUBL, LANES))


def lookup(spread, index):
    rows = spread.shape[1]
    low = index & (LANES - 1)
    high = index >> 7
    bits = [((high >> b) & 1) == 1 for b in range(rows.bit_length() - 1)]
    return [
        select_tree(
            [
                jnp.take_along_axis(spread[c, h], low, axis=1, mode="promise_in_bounds")
                for h in range(rows)
            ],
            bits,
        )
        for c in range(spread.shape[0])
    ]


def interpolate_block(spread, index_ref, weight_ref, o, r, col):
    parts = []
    weights = [
        weight_ref[k, o, pl.ds(r, PACK), pl.ds(col, LANES)].astype(jnp.float32)
        for k in range(index_ref.shape[0])
    ]
    for s in range(0, PACK, SUBL):
        total = None
        for k in range(index_ref.shape[0]):
            found = lookup(spread, index_ref[k, o, pl.ds(r + s, SUBL), pl.ds(col, LANES)])
            w = weights[k][s : s + SUBL]
            terms = [w * v for v in found]
            total = terms if total is None else [a + b for a, b in zip(total, terms)]
        parts.append(total)
    return [jnp.concatenate([p[c] for p in parts], axis=0) for c in range(2)]


def interpolate_kernel(table_ref, index_ref, weight_ref, out_ref, spread):
    spread_table(table_ref, spread)
    _, orients, rows, columns = index_ref.shape
    per_row = columns // LANES
    blocks = rows // PACK * per_row

    def step(i, carry):
        o, rest = i // blocks, i % blocks
        r = pl.multiple_of(rest // per_row * PACK, PACK)
        col = pl.multiple_of(rest % per_row * LANES, LANES)
        found = interpolate_block(spread, index_ref, weight_ref, o, r, col)
        for c in range(2):
            out_ref[c, o, pl.ds(r, PACK), pl.ds(col, LANES)] = found[c].astype(jnp.bfloat16)
        return carry

    lax.fori_loop(0, orients * blocks, step, 0)


def interpolate(interp_index, interp_weight, table):
    _, orients, _, rows, columns = interp_index.shape
    index, weight = interp_index[:, :, 0], interp_weight[:, :, 0]
    short = -rows % PACK
    if short:
        pad = ((0, 0), (0, 0), (0, short), (0, 0))
        index, weight = jnp.pad(index, pad), jnp.pad(weight, pad)
    table = table.astype(jnp.float32).reshape(2, -1, LANES)
    vmem = pl.BlockSpec(memory_space=pltpu.VMEM)
    out = pl.pallas_call(
        interpolate_kernel,
        out_shape=jax.ShapeDtypeStruct((2, orients, rows + short, columns), jnp.bfloat16),
        in_specs=[vmem] * 3,
        out_specs=vmem,
        scratch_shapes=[pltpu.VMEM((2, table.shape[1], SUBL, LANES), jnp.float32)],
        compiler_params=pltpu.CompilerParams(vmem_limit_bytes=32 * 2**20),
        name="interpolate",
    )(table, index, weight)
    return out[:, :, None, :rows]


def angle(turns, length):
    turns = turns - length * jnp.floor((turns + 0.5) * (1.0 / length))
    turns = jnp.where(turns > 0.5 * length, turns - length, turns)
    x = turns * (2.0 * math.pi / length)
    square = x * x
    cosine = jnp.full_like(x, 1.0 / math.factorial(18) * -1.0)
    sine = jnp.full_like(x, 1.0 / math.factorial(17))
    for p in range(16, -1, -2):
        cosine = cosine * square + (-1.0) ** (p // 2) / math.factorial(p)
    for p in range(15, 0, -2):
        sine = sine * square + (-1.0) ** (p // 2) / math.factorial(p)
    return cosine, sine * x


def push(source, target, send, receive, where):
    return pltpu.make_async_remote_copy(
        src_ref=source,
        dst_ref=target,
        send_sem=send,
        recv_sem=receive,
        device_id=where,
        device_id_type=pl.DeviceIdType.MESH,
    )


def fused_kernel(
    sizes,
    table_ref, index_ref, weight_ref, spec_ref, filt_ref, grid_ref,
    count_ref, orient_ref, row_ref, col_ref, forward_hbm, back_hbm, bins_ref,
    maps_ref, refined_ref, best_ref,
    spread, slices, grids, cross, shifted, turn, binned, rows_of, score, scores,
    sent, held, mine, shared, forward, back,
    local_sem, slice_send, slice_recv, grid_send, grid_recv, share_send, share_recv,
    half_send, half_recv, map_send, map_recv, score_send, score_recv,
):
    R, T, N = sizes
    r, t, n = lax.axis_index("rot"), lax.axis_index("tile"), lax.axis_index("nar")
    slots = orient_ref.shape[0]
    half, length = filt_ref.shape
    chunks = index_ref.shape[2] // PACK
    orients = index_ref.shape[1]
    quarter = grid_ref.shape[0] // R
    wide = LANES
    f32, bf16 = jnp.float32, jnp.bfloat16

    barrier = pltpu.get_barrier_semaphore()
    across = [(dr, dn) for dn in range(N) for dr in range(R) if dr or dn]
    along = [(dt, dn) for dn in range(N) for dt in range(T) if dt or dn]

    def rot_nar(dr, dn):
        return {"rot": lax.rem(r + dr, R), "tile": t, "nar": lax.rem(n + dn, N)}

    def tile_nar(dt, dn):
        return {"rot": r, "tile": lax.rem(t + dt, T), "nar": lax.rem(n + dn, N)}

    peers = [rot_nar(*d) for d in across] + [tile_nar(*d) for d in along if d[0]]
    for where in peers:
        pl.semaphore_signal(barrier, inc=1, device_id=where, device_id_type=pl.DeviceIdType.MESH)
    locals_ = [
        pltpu.make_async_copy(forward_hbm, forward, local_sem.at[0]),
        pltpu.make_async_copy(back_hbm, back, local_sem.at[1]),
        pltpu.make_async_copy(grid_ref.at[pl.ds(r * quarter, quarter)], grids.at[r, t], local_sem.at[2]),
    ]
    for copy in locals_:
        copy.start()
    spread_table(table_ref, spread)
    pl.semaphore_wait(barrier, len(peers))

    grid_copies = [
        push(
            grid_ref.at[pl.ds(r * quarter, quarter)], grids.at[r, t],
            grid_send.at[d - 1], grid_recv.at[d - 1], tile_nar(d, 0),
        )
        for d in range(1, T)
    ]
    for copy in grid_copies:
        copy.start()

    ky = lax.broadcasted_iota(jnp.int32, (half, wide), 0) + n * half
    kx = lax.broadcasted_iota(jnp.int32, (PACK, length), 1)
    for i in range(slots):
        c, s = angle((ky * row_ref[i]).astype(f32), length)
        rows_of[0, i], rows_of[1, i] = c, s
        c, s = angle((kx * col_ref[i]).astype(f32), length)
        turn[0, i], turn[1, i] = c, s

    def slice_copy(i, d):
        here = slices.at[t, lax.rem(i, chunks), i // chunks]
        return push(here, here, slice_send.at[i, d - 1], slice_recv.at[i, d - 1], tile_nar(d, 0))

    def form(i, carry):
        o, j = i // chunks, lax.rem(i, chunks)

        def block(b, carry):
            col = pl.multiple_of(b * LANES, LANES)
            first = pl.multiple_of(j * PACK, PACK)
            found = interpolate_block(spread, index_ref, weight_ref, o, first, col)
            for c in range(2):
                slices[t, j, o, c, :, pl.ds(col, LANES)] = found[c].astype(bf16)
            return carry

        lax.fori_loop(0, length // LANES, block, 0)
        for d in range(1, T):
            slice_copy(i, d).start()
        return carry

    total = orients * chunks
    lax.fori_loop(0, total // 2, form, 0)
    for copy in grid_copies:
        copy.wait()
    locals_[2].wait()
    share_copies = [
        push(grids.at[r], grids.at[r], share_send.at[d - 1], share_recv.at[d - 1], rot_nar(d, 0))
        for d in range(1, R)
    ]
    for copy in share_copies:
        copy.start()
    lax.fori_loop(total // 2, total, form, 0)

    def arrived(i, carry):
        for d in range(1, T):
            there = slices.at[lax.rem(t + T - d, T), lax.rem(i, chunks), i // chunks]
            push(there, there, slice_send.at[i, d - 1], slice_recv.at[i, d - 1], tile_nar(d, 0)).wait_recv()
        return carry

    lax.fori_loop(0, total, arrived, 0)

    def product(b, carry):
        blocks = length // LANES
        place = b // blocks
        col = pl.multiple_of(lax.rem(b, blocks) * LANES, LANES)
        first = pl.multiple_of(place * PACK, PACK)
        there, lanes = pl.ds(first, PACK), pl.ds(col, LANES)
        mr, mi = (spec_ref[c, there, lanes].astype(f32) for c in range(2))
        filt = filt_ref[there, lanes].astype(f32)
        plain = []
        for o in range(orients):
            sr, si = (
                slices[place // chunks, lax.rem(place, chunks), o, c, :, lanes].astype(f32)
                for c in range(2)
            )
            cr, ci = filt * sr, filt * si
            xr, xi = mr * cr + mi * ci, mi * cr - mr * ci
            down = pl.ds(pl.multiple_of(o * half + first, PACK), PACK)
            cross[down, lanes] = xr.astype(bf16)
            cross[down, pl.ds(pl.multiple_of(length + col, LANES), LANES)] = xi.astype(bf16)
            pr, pi = mr * sr + mi * si, mi * sr - mr * si
            plain.append((pr.astype(bf16).astype(f32), pi.astype(bf16).astype(f32)))
        for i in range(slots):
            pr, pi = plain[0]
            for o in range(1, orients):
                chosen = orient_ref[i] == o
                pr = jnp.where(chosen, plain[o][0], pr)
                pi = jnp.where(chosen, plain[o][1], pi)
            cc, cs = turn[0, i, :, lanes], turn[1, i, :, lanes]
            rc, rs = rows_of[0, i, there, :], rows_of[1, i, there, :]
            value = rc * (pr * cc - pi * cs) - rs * (pr * cs + pi * cc)
            down = pl.ds(pl.multiple_of(i * half + first, PACK), PACK)
            shifted[down, lanes] = value.astype(bf16)
        return carry

    lax.fori_loop(0, half // PACK * (length // LANES), product, 0)

    locals_[0].wait()
    half_copies = []
    for dn in range(N - 1, -1, -1):
        to_n = lax.rem(n + dn, N)
        full = lax.dot_general(
            forward[to_n], cross[...], (((1,), (1,)), ((), ())), preferred_element_type=f32
        ).astype(bf16)
        sent[dn] = full.reshape(sent.shape[1:])
        for dr in range(R):
            if dr or dn:
                k = dn * R + dr - 1
                copy = push(
                    sent.at[dn, lax.rem(r + dr, R)], held.at[n, :, r],
                    half_send.at[k], half_recv.at[k], rot_nar(dr, dn),
                )
                copy.start()
                half_copies.append((copy, dr, dn))
    for c in range(2):
        held[n, c, r] = sent[0, r, c]

    flat = jnp.dot(shifted[...], bins_ref[...], preferred_element_type=f32)
    for i in range(slots):
        part = flat[i * half : (i + 1) * half].astype(bf16).astype(f32)
        binned[i] = jnp.where(count_ref[0, 0] > i, part, jnp.zeros_like(part))
    for copy in share_copies:
        copy.wait()
    narrow = grids.shape[-1]

    def assess(k, carry):
        a, rest = k // (T * quarter), lax.rem(k, T * quarter)
        b, j = rest // quarter, lax.rem(rest, quarter)
        q = b * (R * quarter) + a * quarter + j
        g = grids[a, b, j].astype(f32)
        for i in range(slots):
            score[i, pl.ds(q, 1), :] = jnp.sum(g * binned[i, :, :narrow], axis=0, keepdims=True)
        return carry

    lax.fori_loop(0, R * T * quarter, assess, 0)
    lane = lax.broadcasted_iota(jnp.int32, scores.shape[2:], 1)
    mixed = jnp.zeros(scores.shape[2:], f32)
    for i in range(slots):
        summed = jnp.sum(score[i], axis=1, keepdims=True) * (1.0 / length)
        mixed = jnp.where(lane == t * slots + i, summed, mixed)
    scores[n, t] = mixed
    score_copies = []
    for k, (dt, dn) in enumerate(along):
        copy = push(scores.at[n, t], scores.at[n, t], score_send.at[k], score_recv.at[k], tile_nar(dt, dn))
        copy.start()
        score_copies.append(copy)

    locals_[1].wait()
    for copy, dr, dn in half_copies:
        there = held.at[lax.rem(n + N - dn, N), :, lax.rem(r + R - dr, R)]
        k = dn * R + dr - 1
        push(there, there, half_send.at[k], half_recv.at[k], rot_nar(dr, dn)).wait_recv()
    corr = None
    for m in range(N):
        for c in range(2):
            part = jnp.dot(
                held[m, c].reshape(-1, held.shape[-1]), back[m, c], preferred_element_type=f32
            )
            corr = part if corr is None else corr + part
    rows = held.shape[3]
    parts = [
        corr[a * rows : (a + 1) * rows, o * length : (o + 1) * length]
        for a in range(R)
        for o in range(orients)
    ]
    top = functools.reduce(jnp.maximum, parts) * (1.0 / length)
    mean = functools.reduce(lambda a, b: a + b, parts) * (1.0 / (length * orients * R))
    shared[r, 0], shared[r, 1] = top.astype(bf16), mean.astype(bf16)
    map_copies = [
        push(shared.at[r], shared.at[r], map_send.at[d - 1], map_recv.at[d - 1], rot_nar(d, 0))
        for d in range(1, R)
    ]
    for copy in map_copies:
        copy.start()

    for k, (dt, dn) in enumerate(along):
        there = scores.at[lax.rem(n + N - dn, N), lax.rem(t + T - dt, T)]
        push(there, there, score_send.at[k], score_recv.at[k], tile_nar(dt, dn)).wait_recv()
    whole = None
    for b in range(T):
        for m in range(N):
            whole = scores[m, b] if whole is None else whole + scores[m, b]
    mine[...] = whole
    best_ref[...] = jnp.max(whole, axis=0, keepdims=True)
    own = refined_ref.shape[0]
    refined_ref[...] = mine[pl.ds(pl.multiple_of(t * own, own), own), :]

    def left(i, carry):
        for d in range(1, T):
            slice_copy(i, d).wait_send()
        return carry

    lax.fori_loop(0, total, left, 0)
    for copy, _, _ in half_copies:
        copy.wait_send()
    for copy in score_copies:
        copy.wait_send()
    for d, copy in enumerate(map_copies, 1):
        there = shared.at[lax.rem(r + R - d, R)]
        push(there, there, map_send.at[d - 1], map_recv.at[d - 1], rot_nar(d, 0)).wait_recv()
    for k in range(2):
        full = jnp.concatenate([shared[a, k].astype(f32) for a in range(R)], axis=0)
        maps_ref[k] = full.T
    for copy in map_copies:
        copy.wait_send()


def constants(length, half, orients, R, N):
    steps = np.arange(length)
    phase = (steps[:, None] * steps[None, :] % length).astype(np.float64) * (2.0 * np.pi / length)
    cosv, sinv = np.cos(phase), np.sin(phase)
    by_x = np.stack([np.concatenate([cosv, -sinv], 0).T, np.concatenate([sinv, cosv], 0).T])
    rows = length // (N * R)
    forward = by_x.reshape(2, N, R, rows, 2 * length).transpose(1, 2, 0, 3, 4)
    forward = forward.reshape(N, R * 2 * rows, 2 * length)
    by_ky = np.stack([cosv, -sinv], 0).reshape(2, N, half, length).transpose(1, 0, 2, 3)
    back = np.zeros((N, 2, orients, half, orients, length))
    for o in range(orients):
        back[:, :, o, :, o, :] = by_ky
    back = back.reshape(N, 2, orients * half, orients * length)
    bins = (steps[:, None] // 4 == np.arange(LANES)[None, :]).astype(np.float32)
    return [jnp.asarray(a.astype(ml_dtypes.bfloat16)) for a in (forward, back, bins)]


def fused(sizes, args):
    (interp_index, interp_weight, volume, spectrum, ctf_filter, peak_count, peak_orient, peak_row,
     peak_col, ctf_grid) = args
    R, T, N = sizes
    _, orients, _, rows, length = interp_index.shape
    half = spectrum.shape[3]
    slots = peak_orient.shape[0]
    defoci = ctf_grid.shape[0]
    chunks = rows // PACK
    share = length // (N * R)
    quarter = defoci // R
    table = volume[:, 0, 0].astype(jnp.float32).reshape(2, -1, LANES)
    forward, back, bins = constants(length, half, orients, R, N)
    grid = ctf_grid[:, 0].reshape(defoci, half, length // 4)
    vmem = pl.BlockSpec(memory_space=pltpu.VMEM)
    smem = pl.BlockSpec(memory_space=pltpu.SMEM)
    hbm = pl.BlockSpec(memory_space=pl.ANY)
    f32, bf16 = jnp.float32, jnp.bfloat16
    total, peers, near = orients * chunks, R * N - 1, T * N - 1
    dma = pltpu.SemaphoreType.DMA
    maps, refined, best = pl.pallas_call(
        functools.partial(fused_kernel, sizes),
        out_shape=(
            jax.ShapeDtypeStruct((2, length, half), f32),
            jax.ShapeDtypeStruct((defoci, LANES), f32),
            jax.ShapeDtypeStruct((1, LANES), f32),
        ),
        in_specs=[vmem] * 6 + [smem] * 4 + [hbm] * 2 + [vmem],
        out_specs=(vmem, vmem, vmem),
        scratch_shapes=[
            pltpu.VMEM((2, table.shape[1], SUBL, LANES), f32),
            pltpu.VMEM((T, chunks, orients, 2, PACK, length), bf16),
            pltpu.VMEM((R, T, quarter, half, length // 4), bf16),
            pltpu.VMEM((orients * half, 2 * length), bf16),
            pltpu.VMEM((slots * half, length), bf16),
            pltpu.VMEM((2, slots, PACK, length), f32),
            pltpu.VMEM((slots, half, LANES), f32),
            pltpu.VMEM((2, slots, half, LANES), f32),
            pltpu.VMEM((slots, T * defoci, length // 4), f32),
            pltpu.VMEM((N, T, T * defoci, LANES), f32),
            pltpu.VMEM((N, R, 2, share, orients * half), bf16),
            pltpu.VMEM((N, 2, R, share, orients * half), bf16),
            pltpu.VMEM((T * defoci, LANES), f32),
            pltpu.VMEM((R, 2, share, length), bf16),
            pltpu.VMEM(forward.shape, bf16),
            pltpu.VMEM(back.shape, bf16),
            dma((3,)),
            dma((total, T - 1)), dma((total, T - 1)),
            dma((T - 1,)), dma((T - 1,)),
            dma((R - 1,)), dma((R - 1,)),
            dma((peers,)), dma((peers,)),
            dma((R - 1,)), dma((R - 1,)),
            dma((near,)), dma((near,)),
        ],
        compiler_params=pltpu.CompilerParams(
            collective_id=0, has_side_effects=True, vmem_limit_bytes=48 * 2**20
        ),
        name="match",
    )(
        table, interp_index[:, :, 0], interp_weight[:, :, 0], spectrum[:, 0, 0], ctf_filter[0, 0],
        grid, peak_count, peak_orient, peak_row, peak_col, forward, back, bins,
    )
    listed = T * slots
    return (
        maps[0].reshape(1, 1, -1),
        maps[1].reshape(1, 1, -1),
        refined[:, :listed].T.reshape(1, listed, defoci),
        best[:, :listed],
    )


def merged(x, axis, combine):
    everything = jax.tree.map(
        lambda part, kind: lax.all_gather(part.astype(kind), axis), x, (jnp.bfloat16, jnp.bfloat16)
    )

    def take(k):
        return jax.tree.map(lambda part, own: part[k].astype(own.dtype), everything, x)

    return lax.fori_loop(
        1, lax.axis_size(axis), lambda k, so_far: combine(so_far, take(k)), take(0)
    )


def dft_tables(length):
    steps = jnp.arange(length, dtype=jnp.int32)
    phase = (steps[:, None] * steps[None, :] % length).astype(jnp.float32) * (2.0 * jnp.pi / length)
    cosv = jnp.cos(phase).astype(jnp.bfloat16)
    sinv = jnp.sin(phase).astype(jnp.bfloat16)
    wide = jnp.concatenate([jnp.concatenate([cosv, sinv], 1), jnp.concatenate([-sinv, cosv], 1)], 0)
    back = jnp.stack([cosv, -sinv], axis=1)
    return (wide, back)


def combine_stats(first, second):
    return (jnp.maximum(first[0], second[0]), first[1] + second[1])


def shards(
    interp_index,
    interp_weight,
    volume,
    spectrum,
    ctf_filter,
    peak_count,
    peak_orient,
    peak_row,
    peak_col,
    ctf_grid,
):
    table = volume[:, 0, 0]
    weighted = interpolate(interp_index, interp_weight, table)
    length = spectrum.shape[4]
    half = spectrum.shape[3]
    orients = weighted.shape[1]
    slots = peak_orient.shape[0]
    wide, back = dft_tables(length)
    spec = spectrum[:, 0, 0]
    filt = ctf_filter[0, 0]
    piece = lax.all_gather(weighted, "tile", axis=3, tiled=True)
    count = piece.shape[3]
    spec_rows = spec.astype(jnp.float32)
    filt_rows = filt.astype(jnp.float32)
    sr = piece[0, :, 0].astype(jnp.float32)
    si = piece[1, :, 0].astype(jnp.float32)
    cr = filt_rows * sr
    ci = filt_rows * si
    xr = spec_rows[0] * cr + spec_rows[1] * ci
    xi = spec_rows[1] * cr - spec_rows[0] * ci
    cross = jnp.stack([xr, xi], axis=2).astype(jnp.bfloat16)
    rows_out = jnp.dot(
        cross.reshape(orients * count, 2 * length), wide, preferred_element_type=jnp.float32
    )
    rows_out = rows_out.astype(jnp.bfloat16).reshape(orients, count, 2, length)
    picked_r = jnp.take(sr, peak_orient, axis=0)
    picked_i = jnp.take(si, peak_orient, axis=0)
    plain_r = spec_rows[0] * picked_r + spec_rows[1] * picked_i
    plain_i = spec_rows[1] * picked_r - spec_rows[0] * picked_i
    plain = jnp.stack([plain_r, plain_i], axis=2).astype(jnp.bfloat16)
    combined = jnp.concatenate([rows_out, plain], axis=0)
    halfimg = combined[:orients]
    plain = combined[orients:].astype(jnp.float32)
    offset = lax.axis_index("nar") * half
    back_rows = lax.dynamic_slice_in_dim(back, offset, half, 2)
    partial_value = jnp.einsum(
        "yck,okcx->oyx", back_rows, halfimg, preferred_element_type=jnp.float32
    )
    summed = lax.psum_scatter(
        partial_value.astype(jnp.bfloat16), "nar", scatter_dimension=2, tiled=True
    ).astype(jnp.float32)
    corr = summed * (1.0 / length)
    local_max = jnp.max(corr, axis=0)
    local_sum = jnp.sum(corr, axis=0)
    group_count = lax.axis_size("rot")
    top, total = merged((local_max, local_sum), "rot", combine_stats)
    mean = total / (orients * group_count)
    freq_rows = lax.axis_index("nar") * half + jnp.arange(half, dtype=jnp.int32)
    freq_cols = jnp.arange(length, dtype=jnp.int32)
    unit = 2.0 * jnp.pi / length
    row_turn = ((freq_rows[None, :] * peak_row[:, None]) % length).astype(jnp.float32) * unit
    col_turn = ((freq_cols[None, :] * peak_col[:, None]) % length).astype(jnp.float32) * unit
    rc, rs = jnp.cos(row_turn)[:, :, None], jnp.sin(row_turn)[:, :, None]
    cc, cs = jnp.cos(col_turn)[:, None, :], jnp.sin(col_turn)[:, None, :]
    shifted = plain[:, :, 0] * (rc * cc - rs * cs) - plain[:, :, 1] * (rs * cc + rc * cs)
    binned = jnp.sum(shifted.reshape(slots, half, length // 4, 4), axis=3).astype(jnp.bfloat16)
    valid = jnp.arange(slots, dtype=jnp.int32) < peak_count[0, 0]
    binned = jnp.where(valid[:, None, None], binned, jnp.zeros_like(binned)).reshape(slots, -1)
    grid_local = ctf_grid[:, 0]
    grid_count = grid_local.shape[0]
    listed = lax.axis_size("tile") * slots
    part = lax.dot_general(
        lax.all_gather(binned, "tile", axis=0, tiled=True),
        grid_local,
        (((1,), (1,)), ((), ())),
        preferred_element_type=jnp.float32,
    )
    refined = lax.psum(part, "nar") * (1.0 / length)
    best = lax.pmax(jnp.max(refined, axis=1), "tile")
    return (
        top.reshape(1, 1, -1),
        mean.reshape(1, 1, -1),
        refined.reshape(1, listed, grid_count),
        best.reshape(1, listed),
    )


def fits(sizes, args):
    R, T, N = sizes
    _, orients, _, rows, length = args[0].shape
    half, slots, defoci = args[3].shape[3], args[6].shape[0], args[9].shape[0]
    return (
        rows % PACK == 0
        and orients * rows // PACK % 2 == 0
        and T <= 8
        and T * rows == half
        and N * half == length
        and length % LANES == 0
        and length % (N * R * PACK) == 0
        and defoci == SUBL
        and defoci % R == 0
        and T * slots <= LANES
        and length // 4 <= LANES
    )


def solution(mesh):
    sizes = tuple(mesh.shape[axis] for axis in ("rot", "tile", "nar"))

    def body(*args):
        return fused(sizes, args) if fits(sizes, args) else shards(*args)

    return jax.shard_map(
        body,
        mesh=mesh,
        in_specs=(
            P(None, "rot", "nar", "tile", None),
            P(None, "rot", "nar", "tile", None),
            P(None, "nar", "tile", None),
            P(None, "tile", "nar", None, None),
            P("tile", "nar", None, None),
            P("rot", "tile"),
            P(("rot", "tile")),
            P(("rot", "tile")),
            P(("rot", "tile")),
            P("tile", "nar", None),
        ),
        out_specs=(
            P("tile", "nar", None),
            P("tile", "nar", None),
            P("rot", None, "tile"),
            P("rot", None),
        ),
        check_vma=False,
    )
```

```python
import functools
import math

import jax
import jax.numpy as jnp
import ml_dtypes
import numpy as np
from jax import lax
from jax.experimental import pallas as pl
from jax.experimental.pallas import tpu as pltpu
from jax.sharding import PartitionSpec as P

LANES = 128
SUBL = 8
PACK = 16


def select_tree(items, bits):
    for bit in bits:
        items = [jnp.where(bit, b, a) for a, b in zip(items[::2], items[1::2])]
    return items[0]


def spread_table(table_ref, spread):
    for h in range(spread.shape[1]):
        both = table_ref[:, h * LANES : (h + 1) * LANES].astype(jnp.float32)
        for c in range(2):
            spread[c, h] = jnp.broadcast_to(both[c : c + 1], (SUBL, LANES))


def lookup(spread, index):
    rows = spread.shape[1]
    low = index & (LANES - 1)
    high = index >> 7
    bits = [((high >> b) & 1) == 1 for b in range(rows.bit_length() - 1)]
    return [
        select_tree(
            [
                jnp.take_along_axis(spread[c, h], low, axis=1, mode="promise_in_bounds")
                for h in range(rows)
            ],
            bits,
        )
        for c in range(spread.shape[0])
    ]


def interpolate_block(spread, index_ref, weight_ref, o, r, col):
    parts = []
    weights = [
        weight_ref[k, o, pl.ds(r, PACK), pl.ds(col, LANES)].astype(jnp.float32)
        for k in range(index_ref.shape[0])
    ]
    for s in range(0, PACK, SUBL):
        total = None
        for k in range(index_ref.shape[0]):
            found = lookup(spread, index_ref[k, o, pl.ds(r + s, SUBL), pl.ds(col, LANES)])
            w = weights[k][s : s + SUBL]
            terms = [w * v for v in found]
            total = terms if total is None else [a + b for a, b in zip(total, terms)]
        parts.append(total)
    return [jnp.concatenate([p[c] for p in parts], axis=0) for c in range(2)]


def interpolate_kernel(table_ref, index_ref, weight_ref, out_ref, spread):
    spread_table(table_ref, spread)
    _, orients, rows, columns = index_ref.shape
    per_row = columns // LANES
    blocks = rows // PACK * per_row

    def step(i, carry):
        o, rest = i // blocks, i % blocks
        r = pl.multiple_of(rest // per_row * PACK, PACK)
        col = pl.multiple_of(rest % per_row * LANES, LANES)
        found = interpolate_block(spread, index_ref, weight_ref, o, r, col)
        for c in range(2):
            out_ref[c, o, pl.ds(r, PACK), pl.ds(col, LANES)] = found[c].astype(jnp.bfloat16)
        return carry

    lax.fori_loop(0, orients * blocks, step, 0)


def interpolate(interp_index, interp_weight, table):
    _, orients, _, rows, columns = interp_index.shape
    index, weight = interp_index[:, :, 0], interp_weight[:, :, 0]
    short = -rows % PACK
    if short:
        pad = ((0, 0), (0, 0), (0, short), (0, 0))
        index, weight = jnp.pad(index, pad), jnp.pad(weight, pad)
    vmem = pl.BlockSpec(memory_space=pltpu.VMEM)
    out = pl.pallas_call(
        interpolate_kernel,
        out_shape=jax.ShapeDtypeStruct((2, orients, rows + short, columns), jnp.bfloat16),
        in_specs=[vmem] * 3,
        out_specs=vmem,
        scratch_shapes=[pltpu.VMEM((2, table.shape[1] // LANES, SUBL, LANES), jnp.float32)],
        compiler_params=pltpu.CompilerParams(vmem_limit_bytes=32 * 2**20),
        name="interpolate",
    )(table, index, weight)
    return out[:, :, None, :rows]


def angle(turns, length):
    turns = turns - length * jnp.floor((turns + 0.5) * (1.0 / length))
    turns = jnp.where(turns > 0.5 * length, turns - length, turns)
    x = turns * (2.0 * math.pi / length)
    square = x * x
    cosine = jnp.full_like(x, 1.0 / math.factorial(18) * -1.0)
    sine = jnp.full_like(x, 1.0 / math.factorial(17))
    for p in range(16, -1, -2):
        cosine = cosine * square + (-1.0) ** (p // 2) / math.factorial(p)
    for p in range(15, 0, -2):
        sine = sine * square + (-1.0) ** (p // 2) / math.factorial(p)
    return cosine, sine * x


def push(source, target, send, receive, where):
    return pltpu.make_async_remote_copy(
        src_ref=source,
        dst_ref=target,
        send_sem=send,
        recv_sem=receive,
        device_id=where,
        device_id_type=pl.DeviceIdType.MESH,
    )


def fused_kernel(
    sizes,
    table_hbm, index_hbm, weight_hbm, spec_hbm, filt_hbm, grid_hbm,
    count_hbm, orient_hbm, row_hbm, col_hbm, forward_hbm, back_hbm, bins_hbm,
    top_ref, mean_ref, refined_ref, best_ref,
    table_ref, index_ref, weight_ref, spec_ref, filt_ref, forward, back, bins_ref,
    count_ref, orient_ref, row_ref, col_ref,
    spread, slices, grids, cross, shifted, turn, binned, rows_of, scores,
    sent, held, mine, shared,
    local_sem, slice_send, slice_recv, grid_send, grid_recv, share_send, share_recv,
    half_send, half_recv, map_send, map_recv, score_send, score_recv,
):
    R, T, N = sizes
    r, t, n = lax.axis_index("rot"), lax.axis_index("tile"), lax.axis_index("nar")
    slots = orient_ref.shape[0]
    half, length = filt_ref.shape
    chunks = index_ref.shape[2] // PACK
    orients = index_ref.shape[1]
    blocks = length // LANES
    span = grids.shape[-1]
    f32, bf16 = jnp.float32, jnp.bfloat16

    barrier = pltpu.get_barrier_semaphore()
    across = [(dr, dn) for dn in range(N - 1, -1, -1) for dr in range(R) if dr or dn]
    along = [(dt, dn) for dn in range(N) for dt in range(T) if dt or dn]

    def rot_nar(dr, dn):
        return {"rot": lax.rem(r + dr, R), "tile": t, "nar": lax.rem(n + dn, N)}

    def tile_nar(dt, dn):
        return {"rot": r, "tile": lax.rem(t + dt, T), "nar": lax.rem(n + dn, N)}

    peers = [rot_nar(*d) for d in across] + [tile_nar(*d) for d in along if d[0]]
    for where in peers:
        pl.semaphore_signal(barrier, inc=1, device_id=where, device_id_type=pl.DeviceIdType.MESH)
    quarter = grid_hbm.at[:, pl.ds(pl.multiple_of(r * span, span), span)]
    pairs = dict(
        table=(table_hbm, table_ref),
        spec=(spec_hbm, spec_ref),
        filt=(filt_hbm, filt_ref),
        grid=(quarter, grids.at[r, t]),
        forward=(forward_hbm, forward),
        count=(count_hbm, count_ref),
        orient=(orient_hbm, orient_ref),
        row=(row_hbm, row_ref),
        col=(col_hbm, col_ref),
        bins=(bins_hbm, bins_ref),
        back=(back_hbm, back),
    )
    for o in range(orients):
        pairs[f"index{o}"] = (index_hbm.at[:, o], index_ref.at[:, o])
        pairs[f"weight{o}"] = (weight_hbm.at[:, o], weight_ref.at[:, o])
    first = ["table", "index0", "weight0"]
    order = first + [name for name in pairs if name not in first]
    inputs = {
        name: pltpu.make_async_copy(*pairs[name], local_sem.at[k]) for k, name in enumerate(order)
    }
    for name in order:
        inputs[name].start()
    inputs["table"].wait()
    spread_table(table_ref, spread)
    pl.semaphore_wait(barrier, len(peers))

    def grid_copy(d):
        return push(quarter, grids.at[r, t], grid_send.at[d - 1], grid_recv.at[d - 1], tile_nar(d, 0))

    def share_copy(d):
        return push(grids.at[r], grids.at[r], share_send.at[d - 1], share_recv.at[d - 1], rot_nar(d, 0))

    for d in range(1, T):
        grid_copy(d).start()

    def slice_copy(i, d):
        here = slices.at[t, lax.rem(i, chunks), i // chunks]
        return push(here, here, slice_send.at[i, d - 1], slice_recv.at[i, d - 1], tile_nar(d, 0))

    def half_copy(o, dr, dn):
        k = dn * R + dr - 1
        return push(
            sent.at[o, dn, lax.rem(r + dr, R)], held.at[n, r, o],
            half_send.at[o, k], half_recv.at[o, k], rot_nar(dr, dn),
        )

    def products(o):
        def arrived(i, carry):
            for d in range(1, T):
                there = slices.at[lax.rem(t + T - d, T), lax.rem(i, chunks), i // chunks]
                push(there, there, slice_send.at[i, d - 1], slice_recv.at[i, d - 1], tile_nar(d, 0)).wait_recv()
            return carry

        lax.fori_loop(o * chunks, (o + 1) * chunks, arrived, 0)

        def product(place, carry):
            down = pl.ds(pl.multiple_of(place * PACK, PACK), PACK)
            for b in range(blocks):
                lanes = slice(b * LANES, (b + 1) * LANES)
                mr, mi = (spec_ref[c, down, lanes].astype(f32) for c in range(2))
                filt = filt_ref[down, lanes].astype(f32)
                sr, si = (
                    slices[place // chunks, lax.rem(place, chunks), o, c, :, lanes].astype(f32)
                    for c in range(2)
                )
                cr, ci = filt * sr, filt * si
                cross[o, down, lanes] = (mr * cr + mi * ci).astype(bf16)
                cross[o, down, length + b * LANES : length + (b + 1) * LANES] = (
                    mi * cr - mr * ci
                ).astype(bf16)
            return carry

        lax.fori_loop(0, half // PACK, product, 0)
        for dn in range(N - 1, -1, -1):
            full = lax.dot_general(
                forward[lax.rem(n + dn, N)], cross[o], (((1,), (1,)), ((), ())),
                preferred_element_type=f32,
            ).astype(bf16)
            sent[o, dn] = full.reshape(sent.shape[2:])
            for dr in range(R):
                if dr or dn:
                    half_copy(o, dr, dn).start()
        held[n, r, o] = sent[o, 0, r]

    total = orients * chunks

    def form(i, carry):
        o, j = i // chunks, lax.rem(i, chunks)
        for k in range(orients):
            @pl.when(i == k * chunks)
            def _():
                inputs[f"index{k}"].wait()
                inputs[f"weight{k}"].wait()

        @pl.when(i == 2)
        def _():
            for d in range(1, T):
                grid_copy(d).wait()
            inputs["grid"].wait()
            for d in range(1, R):
                share_copy(d).start()

        @pl.when(i == total - 1)
        def _():
            inputs["spec"].wait()
            inputs["filt"].wait()
            inputs["forward"].wait()
            for k in range(orients - 1):
                products(k)

        def block(b, carry):
            col = pl.multiple_of(b * LANES, LANES)
            start = pl.multiple_of(j * PACK, PACK)
            found = interpolate_block(spread, index_ref, weight_ref, o, start, col)
            for c in range(2):
                slices[t, j, o, c, :, pl.ds(col, LANES)] = found[c].astype(bf16)
            return carry

        lax.fori_loop(0, blocks, block, 0)
        for d in range(1, T):
            slice_copy(i, d).start()
        return carry

    lax.fori_loop(0, total, form, 0)

    for name in ("count", "orient", "row", "col", "bins", "back"):
        inputs[name].wait()
    ky = lax.broadcasted_iota(jnp.int32, (half, LANES), 0) + n * half
    kx = lax.broadcasted_iota(jnp.int32, (PACK, length), 1)
    for i in range(slots):
        c, s = angle((ky * row_ref[i]).astype(f32), length)
        rows_of[0, i], rows_of[1, i] = c, s
        c, s = angle((kx * col_ref[i]).astype(f32), length)
        turn[0, i], turn[1, i] = c, s

    products(orients - 1)

    def peaks(place, carry):
        down = pl.ds(pl.multiple_of(place * PACK, PACK), PACK)
        for b in range(blocks):
            lanes = slice(b * LANES, (b + 1) * LANES)
            mr, mi = (spec_ref[c, down, lanes].astype(f32) for c in range(2))
            plain = []
            for o in range(orients):
                sr, si = (
                    slices[place // chunks, lax.rem(place, chunks), o, c, :, lanes].astype(f32)
                    for c in range(2)
                )
                pr, pi = mr * sr + mi * si, mi * sr - mr * si
                plain.append((pr.astype(bf16).astype(f32), pi.astype(bf16).astype(f32)))
            for i in range(slots):
                pr, pi = plain[0]
                for o in range(1, orients):
                    chosen = orient_ref[i] == o
                    pr = jnp.where(chosen, plain[o][0], pr)
                    pi = jnp.where(chosen, plain[o][1], pi)
                cc, cs = turn[0, i, :, lanes], turn[1, i, :, lanes]
                rc, rs = rows_of[0, i, down, :], rows_of[1, i, down, :]
                value = rc * (pr * cc - pi * cs) - rs * (pr * cs + pi * cc)
                shifted[b, pl.ds(pl.multiple_of(i * half + place * PACK, PACK), PACK), :] = value
        return carry

    lax.fori_loop(0, half // PACK, peaks, 0)
    group = half // 4
    flat = jnp.concatenate(
        [
            jnp.concatenate(
                [
                    shifted[b, pl.ds(i * half + v, group, stride=4), :].astype(bf16)
                    for v in range(4)
                    for b in range(blocks)
                ],
                axis=1,
            )
            for i in range(slots)
        ],
        axis=0,
    )
    flat = jnp.dot(flat, bins_ref[...], preferred_element_type=f32)
    for i in range(slots):
        part = flat[i * group : (i + 1) * group].astype(bf16).astype(f32)
        part = jnp.where(count_ref[0, 0] > i, part, jnp.zeros_like(part))
        for b in range(blocks):
            binned[i, b] = part[:, b * LANES : (b + 1) * LANES]

    for d in range(1, R):
        share_copy(d).wait()
    per = span // length
    defoci = grids.shape[2]

    def assess(m, acc):
        a, within = m // per, lax.rem(m, per)
        for b in range(blocks):
            lanes = pl.ds(pl.multiple_of(within * length + b * LANES, LANES), LANES)
            g = [grids[a, k, :, lanes].astype(f32) for k in range(T)]
            for i in range(slots):
                row = jnp.broadcast_to(
                    binned[i, b, pl.ds(m, 1), :], (defoci, LANES)
                )
                acc = [
                    value + g[k % T] * row if k // T == i else value for k, value in enumerate(acc)
                ]
        return acc

    acc = lax.fori_loop(0, group, assess, [jnp.zeros((defoci, LANES), f32)] * (slots * T))
    lane = lax.broadcasted_iota(jnp.int32, (defoci, LANES), 1)
    for k in range(T):
        mixed = jnp.zeros((defoci, LANES), f32)
        for i in range(slots):
            summed = jnp.sum(acc[i * T + k], axis=1, keepdims=True) * (1.0 / length)
            mixed = jnp.where(lane == t * slots + i, summed, mixed)
        scores[n, t, k * defoci : (k + 1) * defoci, :] = mixed

    def score_copy(k, dt, dn):
        return push(scores.at[n, t], scores.at[n, t], score_send.at[k], score_recv.at[k], tile_nar(dt, dn))

    for k, d in enumerate(along):
        score_copy(k, *d).start()

    rows = held.shape[4]
    parts = []
    for o in range(orients):
        for dr, dn in across:
            there = held.at[lax.rem(n + N - dn, N), lax.rem(r + R - dr, R), o]
            k = dn * R + dr - 1
            push(there, there, half_send.at[o, k], half_recv.at[o, k], rot_nar(dr, dn)).wait_recv()
        corr = None
        for m in range(N):
            for c in range(2):
                part = jnp.dot(
                    held[m, :, o, c].reshape(R * rows, half), back[m, c], preferred_element_type=f32
                )
                corr = part if corr is None else corr + part
        parts += [corr[a * rows : (a + 1) * rows] for a in range(R)]
    top = functools.reduce(jnp.maximum, parts) * (1.0 / length)
    mean = functools.reduce(lambda a, b: a + b, parts) * (1.0 / (length * orients * R))
    shared[r, 0], shared[r, 1] = top.astype(bf16), mean.astype(bf16)
    map_copies = [
        push(shared.at[r], shared.at[r], map_send.at[d - 1], map_recv.at[d - 1], rot_nar(d, 0))
        for d in range(1, R)
    ]
    for copy in map_copies:
        copy.start()

    for k, (dt, dn) in enumerate(along):
        there = scores.at[lax.rem(n + N - dn, N), lax.rem(t + T - dt, T)]
        push(there, there, score_send.at[k], score_recv.at[k], tile_nar(dt, dn)).wait_recv()
    whole = None
    for b in range(T):
        for m in range(N):
            whole = scores[m, b] if whole is None else whole + scores[m, b]
    mine[...] = whole
    listed = T * slots
    best_ref[...] = jnp.max(whole, axis=0, keepdims=True)[:, :listed]
    refined_ref[...] = mine[pl.ds(pl.multiple_of(t * defoci, defoci), defoci), :].T[:listed]

    def left(i, carry):
        for d in range(1, T):
            slice_copy(i, d).wait_send()
        return carry

    lax.fori_loop(0, total, left, 0)
    for o in range(orients):
        for d in across:
            half_copy(o, *d).wait_send()
    for k, d in enumerate(along):
        score_copy(k, *d).wait_send()
    for d in range(1, R):
        there = shared.at[lax.rem(r + R - d, R)]
        push(there, there, map_send.at[d - 1], map_recv.at[d - 1], rot_nar(d, 0)).wait_recv()
    for k, out_ref in enumerate((top_ref, mean_ref)):
        full = jnp.concatenate([shared[a, k].astype(f32) for a in range(R)], axis=0)
        paired = jnp.concatenate([full[:, :half], full[:, half:]], axis=0).T
        for b in range(blocks):
            out_ref[pl.ds(b, half, stride=blocks), :] = paired[:, b * LANES : (b + 1) * LANES]
    for copy in map_copies:
        copy.wait_send()


def constants(length, half, R, N):
    steps = np.arange(length)
    phase = (steps[:, None] * steps[None, :] % length).astype(np.float64) * (2.0 * np.pi / length)
    cosv, sinv = np.cos(phase), np.sin(phase)
    by_x = np.stack([np.concatenate([cosv, -sinv], 0).T, np.concatenate([sinv, cosv], 0).T])
    rows = length // (N * R)
    forward = by_x.reshape(2, N, R, rows, 2 * length).transpose(1, 2, 0, 3, 4)
    forward = forward.reshape(N, R * 2 * rows, 2 * length)
    back = np.stack([cosv, -sinv], 0).reshape(2, N, half, length // 2, 2)
    back = back.transpose(1, 0, 2, 4, 3).reshape(N, 2, half, length)
    bins = np.zeros((4, length, 4, length // 4))
    for v in range(4):
        bins[v, steps, v, steps // 4] = 1.0
    bins = bins.reshape(4 * length, length)
    return [jnp.asarray(a.astype(ml_dtypes.bfloat16)) for a in (forward, back, bins)]


def fused(sizes, args):
    (interp_index, interp_weight, volume, spectrum, ctf_filter, peak_count, peak_orient, peak_row,
     peak_col, ctf_grid) = args
    R, T, N = sizes
    neighbours, orients, _, rows, length = interp_index.shape
    half = spectrum.shape[3]
    slots = peak_orient.shape[0]
    defoci, _, bins_all = ctf_grid.shape
    chunks = rows // PACK
    share = length // (N * R)
    entries = volume.shape[3]
    forward, back, bins = constants(length, half, R, N)
    vmem = pl.BlockSpec(memory_space=pltpu.VMEM)
    hbm = pl.BlockSpec(memory_space=pl.ANY)
    f32, bf16, i32 = jnp.float32, jnp.bfloat16, jnp.int32
    total, peers, near = orients * chunks, R * N - 1, T * N - 1
    listed = T * slots
    dma = pltpu.SemaphoreType.DMA
    flat = length * half // LANES
    top, mean, refined, best = pl.pallas_call(
        functools.partial(fused_kernel, sizes),
        out_shape=(
            jax.ShapeDtypeStruct((flat, LANES), f32),
            jax.ShapeDtypeStruct((flat, LANES), f32),
            jax.ShapeDtypeStruct((listed, defoci), f32),
            jax.ShapeDtypeStruct((1, listed), f32),
        ),
        in_specs=[hbm] * 13,
        out_specs=(vmem,) * 4,
        scratch_shapes=[
            pltpu.VMEM((2, entries), bf16),
            pltpu.VMEM((neighbours, orients, rows, length), i32),
            pltpu.VMEM((neighbours, orients, rows, length), bf16),
            pltpu.VMEM((2, half, length), bf16),
            pltpu.VMEM((half, length), bf16),
            pltpu.VMEM(forward.shape, bf16),
            pltpu.VMEM(back.shape, bf16),
            pltpu.VMEM(bins.shape, bf16),
            pltpu.SMEM((1, 1), i32),
            pltpu.SMEM((slots,), i32),
            pltpu.SMEM((slots,), i32),
            pltpu.SMEM((slots,), i32),
            pltpu.VMEM((2, entries // LANES, SUBL, LANES), f32),
            pltpu.VMEM((T, chunks, orients, 2, PACK, length), bf16),
            pltpu.VMEM((R, T, defoci, bins_all // R), bf16),
            pltpu.VMEM((orients, half, 2 * length), bf16),
            pltpu.VMEM((length // LANES, slots * half, LANES), f32),
            pltpu.VMEM((2, slots, PACK, length), f32),
            pltpu.VMEM((slots, length // LANES, half // 4, LANES), f32),
            pltpu.VMEM((2, slots, half, LANES), f32),
            pltpu.VMEM((N, T, T * defoci, LANES), f32),
            pltpu.VMEM((orients, N, R, 2, share, half), bf16),
            pltpu.VMEM((N, R, orients, 2, share, half), bf16),
            pltpu.VMEM((T * defoci, LANES), f32),
            pltpu.VMEM((R, 2, share, length), bf16),
            dma((11 + 2 * orients,)),
            dma((total, T - 1)), dma((total, T - 1)),
            dma((T - 1,)), dma((T - 1,)),
            dma((R - 1,)), dma((R - 1,)),
            dma((orients, peers)), dma((orients, peers)),
            dma((R - 1,)), dma((R - 1,)),
            dma((near,)), dma((near,)),
        ],
        compiler_params=pltpu.CompilerParams(
            collective_id=0, has_side_effects=True, vmem_limit_bytes=60 * 2**20
        ),
        name="match",
    )(
        volume[:, 0, 0], interp_index[:, :, 0], interp_weight[:, :, 0], spectrum[:, 0, 0],
        ctf_filter[0, 0], ctf_grid[:, 0], peak_count, peak_orient, peak_row, peak_col,
        forward, back, bins,
    )
    return (
        top.reshape(1, 1, -1),
        mean.reshape(1, 1, -1),
        refined.reshape(1, listed, defoci),
        best,
    )


def merged(x, axis, combine):
    everything = jax.tree.map(
        lambda part, kind: lax.all_gather(part.astype(kind), axis), x, (jnp.bfloat16, jnp.bfloat16)
    )

    def take(k):
        return jax.tree.map(lambda part, own: part[k].astype(own.dtype), everything, x)

    return lax.fori_loop(
        1, lax.axis_size(axis), lambda k, so_far: combine(so_far, take(k)), take(0)
    )


def dft_tables(length):
    steps = jnp.arange(length, dtype=jnp.int32)
    phase = (steps[:, None] * steps[None, :] % length).astype(jnp.float32) * (2.0 * jnp.pi / length)
    cosv = jnp.cos(phase).astype(jnp.bfloat16)
    sinv = jnp.sin(phase).astype(jnp.bfloat16)
    wide = jnp.concatenate([jnp.concatenate([cosv, sinv], 1), jnp.concatenate([-sinv, cosv], 1)], 0)
    back = jnp.stack([cosv, -sinv], axis=1)
    return (wide, back)


def combine_stats(first, second):
    return (jnp.maximum(first[0], second[0]), first[1] + second[1])


def shards(
    interp_index,
    interp_weight,
    volume,
    spectrum,
    ctf_filter,
    peak_count,
    peak_orient,
    peak_row,
    peak_col,
    ctf_grid,
):
    table = volume[:, 0, 0]
    weighted = interpolate(interp_index, interp_weight, table)
    length = spectrum.shape[4]
    half = spectrum.shape[3]
    orients = weighted.shape[1]
    slots = peak_orient.shape[0]
    wide, back = dft_tables(length)
    spec = spectrum[:, 0, 0]
    filt = ctf_filter[0, 0]
    piece = lax.all_gather(weighted, "tile", axis=3, tiled=True)
    count = piece.shape[3]
    spec_rows = spec.astype(jnp.float32)
    filt_rows = filt.astype(jnp.float32)
    sr = piece[0, :, 0].astype(jnp.float32)
    si = piece[1, :, 0].astype(jnp.float32)
    cr = filt_rows * sr
    ci = filt_rows * si
    xr = spec_rows[0] * cr + spec_rows[1] * ci
    xi = spec_rows[1] * cr - spec_rows[0] * ci
    cross = jnp.stack([xr, xi], axis=2).astype(jnp.bfloat16)
    rows_out = jnp.dot(
        cross.reshape(orients * count, 2 * length), wide, preferred_element_type=jnp.float32
    )
    rows_out = rows_out.astype(jnp.bfloat16).reshape(orients, count, 2, length)
    picked_r = jnp.take(sr, peak_orient, axis=0)
    picked_i = jnp.take(si, peak_orient, axis=0)
    plain_r = spec_rows[0] * picked_r + spec_rows[1] * picked_i
    plain_i = spec_rows[1] * picked_r - spec_rows[0] * picked_i
    plain = jnp.stack([plain_r, plain_i], axis=2).astype(jnp.bfloat16)
    combined = jnp.concatenate([rows_out, plain], axis=0)
    halfimg = combined[:orients]
    plain = combined[orients:].astype(jnp.float32)
    offset = lax.axis_index("nar") * half
    back_rows = lax.dynamic_slice_in_dim(back, offset, half, 2)
    partial_value = jnp.einsum(
        "yck,okcx->oyx", back_rows, halfimg, preferred_element_type=jnp.float32
    )
    summed = lax.psum_scatter(
        partial_value.astype(jnp.bfloat16), "nar", scatter_dimension=2, tiled=True
    ).astype(jnp.float32)
    corr = summed * (1.0 / length)
    local_max = jnp.max(corr, axis=0)
    local_sum = jnp.sum(corr, axis=0)
    group_count = lax.axis_size("rot")
    top, total = merged((local_max, local_sum), "rot", combine_stats)
    mean = total / (orients * group_count)
    freq_rows = lax.axis_index("nar") * half + jnp.arange(half, dtype=jnp.int32)
    freq_cols = jnp.arange(length, dtype=jnp.int32)
    unit = 2.0 * jnp.pi / length
    row_turn = ((freq_rows[None, :] * peak_row[:, None]) % length).astype(jnp.float32) * unit
    col_turn = ((freq_cols[None, :] * peak_col[:, None]) % length).astype(jnp.float32) * unit
    rc, rs = jnp.cos(row_turn)[:, :, None], jnp.sin(row_turn)[:, :, None]
    cc, cs = jnp.cos(col_turn)[:, None, :], jnp.sin(col_turn)[:, None, :]
    shifted = plain[:, :, 0] * (rc * cc - rs * cs) - plain[:, :, 1] * (rs * cc + rc * cs)
    binned = jnp.sum(shifted.reshape(slots, half, length // 4, 4), axis=3).astype(jnp.bfloat16)
    valid = jnp.arange(slots, dtype=jnp.int32) < peak_count[0, 0]
    binned = jnp.where(valid[:, None, None], binned, jnp.zeros_like(binned)).reshape(slots, -1)
    grid_local = ctf_grid[:, 0]
    grid_count = grid_local.shape[0]
    listed = lax.axis_size("tile") * slots
    part = lax.dot_general(
        lax.all_gather(binned, "tile", axis=0, tiled=True),
        grid_local,
        (((1,), (1,)), ((), ())),
        preferred_element_type=jnp.float32,
    )
    refined = lax.psum(part, "nar") * (1.0 / length)
    best = lax.pmax(jnp.max(refined, axis=1), "tile")
    return (
        top.reshape(1, 1, -1),
        mean.reshape(1, 1, -1),
        refined.reshape(1, listed, grid_count),
        best.reshape(1, listed),
    )


def fits(sizes, args):
    R, T, N = sizes
    _, orients, _, rows, length = args[0].shape
    half, slots, defoci = args[3].shape[3], args[6].shape[0], args[9].shape[0]
    return (
        rows % PACK == 0
        and orients * rows // PACK % 2 == 0
        and T <= 8
        and T * rows == half
        and N * half == length
        and length % LANES == 0
        and length % (N * R * PACK) == 0
        and defoci == SUBL
        and defoci % R == 0
        and T * slots <= LANES
        and length // 4 <= LANES
        and args[9].shape[2] == half * (length // 4)
        and args[9].shape[2] % (R * length) == 0
    )


def solution(mesh):
    sizes = tuple(mesh.shape[axis] for axis in ("rot", "tile", "nar"))

    def body(*args):
        return fused(sizes, args) if fits(sizes, args) else shards(*args)

    return jax.shard_map(
        body,
        mesh=mesh,
        in_specs=(
            P(None, "rot", "nar", "tile", None),
            P(None, "rot", "nar", "tile", None),
            P(None, "nar", "tile", None),
            P(None, "tile", "nar", None, None),
            P("tile", "nar", None, None),
            P("rot", "tile"),
            P(("rot", "tile")),
            P(("rot", "tile")),
            P(("rot", "tile")),
            P("tile", "nar", None),
        ),
        out_specs=(
            P("tile", "nar", None),
            P("tile", "nar", None),
            P("rot", None, "tile"),
            P("rot", None),
        ),
        check_vma=False,
    )
```

```python
import functools
import math

import jax
import jax.numpy as jnp
import ml_dtypes
import numpy as np
from jax import lax
from jax.experimental import pallas as pl
from jax.experimental.pallas import tpu as pltpu
from jax.sharding import PartitionSpec as P

LANES = 128
SUBL = 8
PACK = 16


def select_tree(items, bits):
    for bit in bits:
        items = [jnp.where(bit, b, a) for a, b in zip(items[::2], items[1::2])]
    return items[0]


def encode(values):
    rest = jnp.abs(values) * 0.125
    exponent = jnp.zeros_like(rest)
    for step in (64, 32, 16, 8, 4, 2, 1):
        small = rest < 2.0**-step
        rest = jnp.where(small, rest * 2.0**step, rest)
        exponent = jnp.where(small, exponent + step, exponent)
    mantissa = jnp.floor(rest * 256.0)
    mantissa = jnp.where(values < 0, -mantissa, mantissa)
    return (mantissa * 128.0 + exponent).astype(jnp.int32)


def decode(code):
    scale = jnp.exp2(-5.0 - (code & 127).astype(jnp.float32))
    return (code >> 7).astype(jnp.float32) * scale


def spread_table(table_ref, spread):
    for h in range(spread.shape[0]):
        code = encode(table_ref[:, h * LANES : (h + 1) * LANES].astype(jnp.float32))
        word = code[0:1] * 65536 + (code[1:2] & 65535)
        spread[h] = jnp.broadcast_to(word, (SUBL, LANES))


def lookup(spread, index):
    rows = spread.shape[0]
    low = index & (LANES - 1)
    high = index >> 7
    bits = [((high >> b) & 1) == 1 for b in range(rows.bit_length() - 1)]
    word = select_tree(
        [
            jnp.take_along_axis(spread[h], low, axis=1, mode="promise_in_bounds")
            for h in range(rows)
        ],
        bits,
    )
    return [decode(word >> 16), decode((word << 16) >> 16)]


def interpolate_block(spread, index_ref, weight_ref, o, r, col):
    parts = []
    weights = [
        weight_ref[k, o, pl.ds(r, PACK), pl.ds(col, LANES)].astype(jnp.float32)
        for k in range(index_ref.shape[0])
    ]
    for s in range(0, PACK, SUBL):
        total = None
        for k in range(index_ref.shape[0]):
            found = lookup(spread, index_ref[k, o, pl.ds(r + s, SUBL), pl.ds(col, LANES)])
            w = weights[k][s : s + SUBL]
            terms = [w * v for v in found]
            total = terms if total is None else [a + b for a, b in zip(total, terms)]
        parts.append(total)
    return [jnp.concatenate([p[c] for p in parts], axis=0) for c in range(2)]


def interpolate_kernel(table_ref, index_ref, weight_ref, out_ref, spread):
    spread_table(table_ref, spread)
    _, orients, rows, columns = index_ref.shape
    per_row = columns // LANES
    blocks = rows // PACK * per_row

    def step(i, carry):
        o, rest = i // blocks, i % blocks
        r = pl.multiple_of(rest // per_row * PACK, PACK)
        col = pl.multiple_of(rest % per_row * LANES, LANES)
        found = interpolate_block(spread, index_ref, weight_ref, o, r, col)
        for c in range(2):
            out_ref[c, o, pl.ds(r, PACK), pl.ds(col, LANES)] = found[c].astype(jnp.bfloat16)
        return carry

    lax.fori_loop(0, orients * blocks, step, 0)


def interpolate(interp_index, interp_weight, table):
    _, orients, _, rows, columns = interp_index.shape
    index, weight = interp_index[:, :, 0], interp_weight[:, :, 0]
    short = -rows % PACK
    if short:
        pad = ((0, 0), (0, 0), (0, short), (0, 0))
        index, weight = jnp.pad(index, pad), jnp.pad(weight, pad)
    vmem = pl.BlockSpec(memory_space=pltpu.VMEM)
    out = pl.pallas_call(
        interpolate_kernel,
        out_shape=jax.ShapeDtypeStruct((2, orients, rows + short, columns), jnp.bfloat16),
        in_specs=[vmem] * 3,
        out_specs=vmem,
        scratch_shapes=[pltpu.VMEM((table.shape[1] // LANES, SUBL, LANES), jnp.int32)],
        compiler_params=pltpu.CompilerParams(vmem_limit_bytes=32 * 2**20),
        name="interpolate",
    )(table, index, weight)
    return out[:, :, None, :rows]


def angle(turns, length):
    turns = turns - length * jnp.floor((turns + 0.5) * (1.0 / length))
    turns = jnp.where(turns > 0.5 * length, turns - length, turns)
    x = turns * (2.0 * math.pi / length)
    square = x * x
    cosine = jnp.full_like(x, 1.0 / math.factorial(18) * -1.0)
    sine = jnp.full_like(x, 1.0 / math.factorial(17))
    for p in range(16, -1, -2):
        cosine = cosine * square + (-1.0) ** (p // 2) / math.factorial(p)
    for p in range(15, 0, -2):
        sine = sine * square + (-1.0) ** (p // 2) / math.factorial(p)
    return cosine, sine * x


def push(source, target, send, receive, where):
    return pltpu.make_async_remote_copy(
        src_ref=source,
        dst_ref=target,
        send_sem=send,
        recv_sem=receive,
        device_id=where,
        device_id_type=pl.DeviceIdType.MESH,
    )


def fused_kernel(
    sizes,
    table_hbm, index_hbm, weight_hbm, spec_hbm, filt_hbm, grid_hbm,
    count_hbm, orient_hbm, row_hbm, col_hbm, forward_hbm, back_hbm, bins_hbm,
    top_ref, added_ref, refined_ref, best_ref,
    table_ref, index_ref, weight_ref, spec_ref, filt_ref, forward, back, bins_ref,
    count_ref, orient_ref, row_ref, col_ref,
    spread, slices, grids, cross, shifted, turn, binned, rows_of, scores,
    sent, held, mine, shared,
    local_sem, slice_send, slice_recv, grid_send, grid_recv, share_send, share_recv,
    half_send, half_recv, map_send, map_recv, score_send, score_recv,
):
    R, T, N = sizes
    r, t, n = lax.axis_index("rot"), lax.axis_index("tile"), lax.axis_index("nar")
    slots = orient_ref.shape[0]
    half, length = filt_ref.shape
    chunks = index_ref.shape[2] // PACK
    orients = index_ref.shape[1]
    blocks = length // LANES
    span = grids.shape[-1]
    f32, bf16 = jnp.float32, jnp.bfloat16

    barrier = pltpu.get_barrier_semaphore()
    across = [(dr, dn) for dn in range(N - 1, -1, -1) for dr in range(R) if dr or dn]
    along = [(dt, dn) for dn in range(N) for dt in range(T) if dt or dn]

    def rot_nar(dr, dn):
        return {"rot": lax.rem(r + dr, R), "tile": t, "nar": lax.rem(n + dn, N)}

    def tile_nar(dt, dn):
        return {"rot": r, "tile": lax.rem(t + dt, T), "nar": lax.rem(n + dn, N)}

    peers = [rot_nar(*d) for d in across] + [tile_nar(*d) for d in along if d[0]]
    for where in peers:
        pl.semaphore_signal(barrier, inc=1, device_id=where, device_id_type=pl.DeviceIdType.MESH)
    quarter = grid_hbm.at[:, pl.ds(pl.multiple_of(r * span, span), span)]
    pairs = dict(
        table=(table_hbm, table_ref),
        spec=(spec_hbm, spec_ref),
        filt=(filt_hbm, filt_ref),
        grid=(quarter, grids.at[r, t]),
        forward=(forward_hbm, forward),
        count=(count_hbm, count_ref),
        orient=(orient_hbm, orient_ref),
        row=(row_hbm, row_ref),
        col=(col_hbm, col_ref),
        bins=(bins_hbm, bins_ref),
        back=(back_hbm, back),
    )
    for o in range(orients):
        pairs[f"index{o}"] = (index_hbm.at[:, o], index_ref.at[:, o])
        pairs[f"weight{o}"] = (weight_hbm.at[:, o], weight_ref.at[:, o])
    first = ["table", "index0", "weight0"]
    order = first + [name for name in pairs if name not in first]
    inputs = {
        name: pltpu.make_async_copy(*pairs[name], local_sem.at[k]) for k, name in enumerate(order)
    }
    for name in order:
        inputs[name].start()
    inputs["table"].wait()
    spread_table(table_ref, spread)
    pl.semaphore_wait(barrier, len(peers))

    def grid_copy(d):
        return push(quarter, grids.at[r, t], grid_send.at[d - 1], grid_recv.at[d - 1], tile_nar(d, 0))

    def share_copy(d):
        return push(grids.at[r], grids.at[r], share_send.at[d - 1], share_recv.at[d - 1], rot_nar(d, 0))

    for d in range(1, T):
        grid_copy(d).start()

    def slice_copy(i, d):
        here = slices.at[t, lax.rem(i, chunks), i // chunks]
        return push(here, here, slice_send.at[i, d - 1], slice_recv.at[i, d - 1], tile_nar(d, 0))

    def half_copy(o, dr, dn):
        k = dn * R + dr - 1
        return push(
            sent.at[o, dn, lax.rem(r + dr, R)], held.at[n, r, o],
            half_send.at[o, k], half_recv.at[o, k], rot_nar(dr, dn),
        )

    def products(o):
        def arrived(i, carry):
            for d in range(1, T):
                there = slices.at[lax.rem(t + T - d, T), lax.rem(i, chunks), i // chunks]
                push(there, there, slice_send.at[i, d - 1], slice_recv.at[i, d - 1], tile_nar(d, 0)).wait_recv()
            return carry

        lax.fori_loop(o * chunks, (o + 1) * chunks, arrived, 0)

        def product(place, carry):
            down = pl.ds(pl.multiple_of(place * PACK, PACK), PACK)
            for b in range(blocks):
                lanes = slice(b * LANES, (b + 1) * LANES)
                mr, mi = (spec_ref[c, down, lanes].astype(f32) for c in range(2))
                filt = filt_ref[down, lanes].astype(f32)
                sr, si = (
                    slices[place // chunks, lax.rem(place, chunks), o, c, :, lanes].astype(f32)
                    for c in range(2)
                )
                cr, ci = filt * sr, filt * si
                cross[o, down, lanes] = (mr * cr + mi * ci).astype(bf16)
                cross[o, down, length + b * LANES : length + (b + 1) * LANES] = (
                    mi * cr - mr * ci
                ).astype(bf16)
            return carry

        lax.fori_loop(0, half // PACK, product, 0)
        for dn in range(N - 1, -1, -1):
            full = lax.dot_general(
                forward[lax.rem(n + dn, N)], cross[o], (((1,), (1,)), ((), ())),
                preferred_element_type=f32,
            ).astype(bf16)
            sent[o, dn] = full.reshape(sent.shape[2:])
            for dr in range(R):
                if dr or dn:
                    half_copy(o, dr, dn).start()
        held[n, r, o] = sent[o, 0, r]

    total = orients * chunks

    def form(i, carry):
        o, j = i // chunks, lax.rem(i, chunks)
        for k in range(orients):
            @pl.when(i == k * chunks)
            def _():
                inputs[f"index{k}"].wait()
                inputs[f"weight{k}"].wait()

        @pl.when(i == total - 2)
        def _():
            for d in range(1, T):
                grid_copy(d).wait()
            inputs["grid"].wait()
            for d in range(1, R):
                share_copy(d).start()

        def block(b, carry):
            col = pl.multiple_of(b * LANES, LANES)
            start = pl.multiple_of(j * PACK, PACK)
            found = interpolate_block(spread, index_ref, weight_ref, o, start, col)
            for c in range(2):
                slices[t, j, o, c, :, pl.ds(col, LANES)] = found[c].astype(bf16)
            return carry

        lax.fori_loop(0, blocks, block, 0)
        for d in range(1, T):
            slice_copy(i, d).start()
        return carry

    lax.fori_loop(0, total, form, 0)

    for name in ("spec", "filt", "forward", "count", "orient", "row", "col", "bins", "back"):
        inputs[name].wait()
    ky = lax.broadcasted_iota(jnp.int32, (half, LANES), 0) + n * half
    kx = lax.broadcasted_iota(jnp.int32, (PACK, length), 1)
    for i in range(slots):
        c, s = angle((ky * row_ref[i]).astype(f32), length)
        rows_of[0, i], rows_of[1, i] = c, s
        c, s = angle((kx * col_ref[i]).astype(f32), length)
        turn[0, i], turn[1, i] = c, s

    for o in range(orients):
        products(o)

    def peaks(place, carry):
        down = pl.ds(pl.multiple_of(place * PACK, PACK), PACK)
        for b in range(blocks):
            lanes = slice(b * LANES, (b + 1) * LANES)
            mr, mi = (spec_ref[c, down, lanes].astype(f32) for c in range(2))
            plain = []
            for o in range(orients):
                sr, si = (
                    slices[place // chunks, lax.rem(place, chunks), o, c, :, lanes].astype(f32)
                    for c in range(2)
                )
                pr, pi = mr * sr + mi * si, mi * sr - mr * si
                plain.append((pr.astype(bf16).astype(f32), pi.astype(bf16).astype(f32)))
            for i in range(slots):
                pr, pi = plain[0]
                for o in range(1, orients):
                    chosen = orient_ref[i] == o
                    pr = jnp.where(chosen, plain[o][0], pr)
                    pi = jnp.where(chosen, plain[o][1], pi)
                cc, cs = turn[0, i, :, lanes], turn[1, i, :, lanes]
                rc, rs = rows_of[0, i, down, :], rows_of[1, i, down, :]
                value = rc * (pr * cc - pi * cs) - rs * (pr * cs + pi * cc)
                shifted[b, pl.ds(pl.multiple_of(i * half + place * PACK, PACK), PACK), :] = value
        return carry

    lax.fori_loop(0, half // PACK, peaks, 0)
    group = half // 4
    flat = jnp.concatenate(
        [
            jnp.concatenate(
                [
                    shifted[b, pl.ds(i * half + v, group, stride=4), :].astype(bf16)
                    for v in range(4)
                    for b in range(blocks)
                ],
                axis=1,
            )
            for i in range(slots)
        ],
        axis=0,
    )
    flat = jnp.dot(flat, bins_ref[...], preferred_element_type=f32)
    for i in range(slots):
        part = flat[i * group : (i + 1) * group].astype(bf16).astype(f32)
        part = jnp.where(count_ref[0, 0] > i, part, jnp.zeros_like(part))
        for b in range(blocks):
            binned[i, b] = part[:, b * LANES : (b + 1) * LANES]

    for d in range(1, R):
        share_copy(d).wait()
    per = span // length
    defoci = grids.shape[2]

    def assess(m, acc):
        a, within = m // per, lax.rem(m, per)
        for b in range(blocks):
            lanes = pl.ds(pl.multiple_of(within * length + b * LANES, LANES), LANES)
            g = [grids[a, k, :, lanes].astype(f32) for k in range(T)]
            for i in range(slots):
                row = jnp.broadcast_to(
                    binned[i, b, pl.ds(m, 1), :], (defoci, LANES)
                )
                acc = [
                    value + g[k % T] * row if k // T == i else value for k, value in enumerate(acc)
                ]
        return acc

    acc = lax.fori_loop(0, group, assess, [jnp.zeros((defoci, LANES), f32)] * (slots * T))
    lane = lax.broadcasted_iota(jnp.int32, (defoci, LANES), 1)
    for k in range(T):
        mixed = jnp.zeros((defoci, LANES), f32)
        for i in range(slots):
            summed = jnp.sum(acc[i * T + k], axis=1, keepdims=True)
            mixed = jnp.where(lane == t * slots + i, summed, mixed)
        scores[n, t, k * defoci : (k + 1) * defoci, :] = mixed

    def score_copy(k, dt, dn):
        return push(scores.at[n, t], scores.at[n, t], score_send.at[k], score_recv.at[k], tile_nar(dt, dn))

    for k, d in enumerate(along):
        score_copy(k, *d).start()

    rows = held.shape[4]
    parts = []
    for o in range(orients):
        for dr, dn in across:
            there = held.at[lax.rem(n + N - dn, N), lax.rem(r + R - dr, R), o]
            k = dn * R + dr - 1
            push(there, there, half_send.at[o, k], half_recv.at[o, k], rot_nar(dr, dn)).wait_recv()
        corr = None
        for m in range(N):
            for c in range(2):
                part = jnp.dot(
                    held[m, :, o, c].reshape(R * rows, half), back[m, c], preferred_element_type=f32
                )
                corr = part if corr is None else corr + part
        parts += [corr[a * rows : (a + 1) * rows] for a in range(R)]
    top = functools.reduce(jnp.maximum, parts)
    added = functools.reduce(lambda a, b: a + b, parts)
    shared[r, 0], shared[r, 1] = top.astype(bf16), added.astype(bf16)
    map_copies = [
        push(shared.at[r], shared.at[r], map_send.at[d - 1], map_recv.at[d - 1], rot_nar(d, 0))
        for d in range(1, R)
    ]
    for copy in map_copies:
        copy.start()

    for k, (dt, dn) in enumerate(along):
        there = scores.at[lax.rem(n + N - dn, N), lax.rem(t + T - dt, T)]
        push(there, there, score_send.at[k], score_recv.at[k], tile_nar(dt, dn)).wait_recv()
    whole = None
    for b in range(T):
        for m in range(N):
            whole = scores[m, b] if whole is None else whole + scores[m, b]
    mine[...] = whole
    listed = T * slots
    best_ref[...] = jnp.max(whole, axis=0, keepdims=True)[:, :listed]
    refined_ref[...] = mine[pl.ds(pl.multiple_of(t * defoci, defoci), defoci), :][:, :listed]

    def left(i, carry):
        for d in range(1, T):
            slice_copy(i, d).wait_send()
        return carry

    lax.fori_loop(0, total, left, 0)
    for o in range(orients):
        for d in across:
            half_copy(o, *d).wait_send()
    for k, d in enumerate(along):
        score_copy(k, *d).wait_send()
    for d in range(1, R):
        there = shared.at[lax.rem(r + R - d, R)]
        push(there, there, map_send.at[d - 1], map_recv.at[d - 1], rot_nar(d, 0)).wait_recv()
    for k, out_ref in enumerate((top_ref, added_ref)):
        full = jnp.concatenate([shared[a, k].astype(f32) for a in range(R)], axis=0)
        paired = jnp.concatenate([full[:, :half], full[:, half:]], axis=0).T
        for b in range(blocks):
            out_ref[pl.ds(b, half, stride=blocks), :] = paired[:, b * LANES : (b + 1) * LANES]
    for copy in map_copies:
        copy.wait_send()


def constants(length, half, R, N):
    steps = np.arange(length)
    phase = (steps[:, None] * steps[None, :] % length).astype(np.float64) * (2.0 * np.pi / length)
    cosv, sinv = np.cos(phase), np.sin(phase)
    by_x = np.stack([np.concatenate([cosv, -sinv], 0).T, np.concatenate([sinv, cosv], 0).T])
    rows = length // (N * R)
    forward = by_x.reshape(2, N, R, rows, 2 * length).transpose(1, 2, 0, 3, 4)
    forward = forward.reshape(N, R * 2 * rows, 2 * length)
    back = np.stack([cosv, -sinv], 0).reshape(2, N, half, length // 2, 2)
    back = back.transpose(1, 0, 2, 4, 3).reshape(N, 2, half, length)
    bins = np.zeros((4, length, 4, length // 4))
    for v in range(4):
        bins[v, steps, v, steps // 4] = 1.0
    bins = bins.reshape(4 * length, length)
    return [jnp.asarray(a.astype(ml_dtypes.bfloat16)) for a in (forward, back, bins)]


def fused(sizes, args):
    (interp_index, interp_weight, volume, spectrum, ctf_filter, peak_count, peak_orient, peak_row,
     peak_col, ctf_grid) = args
    R, T, N = sizes
    neighbours, orients, _, rows, length = interp_index.shape
    half = spectrum.shape[3]
    slots = peak_orient.shape[0]
    defoci, _, bins_all = ctf_grid.shape
    chunks = rows // PACK
    share = length // (N * R)
    entries = volume.shape[3]
    forward, back, bins = constants(length, half, R, N)
    vmem = pl.BlockSpec(memory_space=pltpu.VMEM)
    hbm = pl.BlockSpec(memory_space=pl.ANY)
    f32, bf16, i32 = jnp.float32, jnp.bfloat16, jnp.int32
    total, peers, near = orients * chunks, R * N - 1, T * N - 1
    listed = T * slots
    dma = pltpu.SemaphoreType.DMA
    flat = length * half // LANES
    top, added, refined, best = pl.pallas_call(
        functools.partial(fused_kernel, sizes),
        out_shape=(
            jax.ShapeDtypeStruct((flat, LANES), f32),
            jax.ShapeDtypeStruct((flat, LANES), f32),
            jax.ShapeDtypeStruct((defoci, listed), f32),
            jax.ShapeDtypeStruct((1, listed), f32),
        ),
        in_specs=[hbm] * 13,
        out_specs=(vmem,) * 4,
        scratch_shapes=[
            pltpu.VMEM((2, entries), bf16),
            pltpu.VMEM((neighbours, orients, rows, length), i32),
            pltpu.VMEM((neighbours, orients, rows, length), bf16),
            pltpu.VMEM((2, half, length), bf16),
            pltpu.VMEM((half, length), bf16),
            pltpu.VMEM(forward.shape, bf16),
            pltpu.VMEM(back.shape, bf16),
            pltpu.VMEM(bins.shape, bf16),
            pltpu.SMEM((1, 1), i32),
            pltpu.SMEM((slots,), i32),
            pltpu.SMEM((slots,), i32),
            pltpu.SMEM((slots,), i32),
            pltpu.VMEM((entries // LANES, SUBL, LANES), i32),
            pltpu.VMEM((T, chunks, orients, 2, PACK, length), bf16),
            pltpu.VMEM((R, T, defoci, bins_all // R), bf16),
            pltpu.VMEM((orients, half, 2 * length), bf16),
            pltpu.VMEM((length // LANES, slots * half, LANES), f32),
            pltpu.VMEM((2, slots, PACK, length), f32),
            pltpu.VMEM((slots, length // LANES, half // 4, LANES), f32),
            pltpu.VMEM((2, slots, half, LANES), f32),
            pltpu.VMEM((N, T, T * defoci, LANES), f32),
            pltpu.VMEM((orients, N, R, 2, share, half), bf16),
            pltpu.VMEM((N, R, orients, 2, share, half), bf16),
            pltpu.VMEM((T * defoci, LANES), f32),
            pltpu.VMEM((R, 2, share, length), bf16),
            dma((11 + 2 * orients,)),
            dma((total, T - 1)), dma((total, T - 1)),
            dma((T - 1,)), dma((T - 1,)),
            dma((R - 1,)), dma((R - 1,)),
            dma((orients, peers)), dma((orients, peers)),
            dma((R - 1,)), dma((R - 1,)),
            dma((near,)), dma((near,)),
        ],
        compiler_params=pltpu.CompilerParams(
            collective_id=0, has_side_effects=True, vmem_limit_bytes=60 * 2**20
        ),
        name="match",
    )(
        volume[:, 0, 0], interp_index[:, :, 0], interp_weight[:, :, 0], spectrum[:, 0, 0],
        ctf_filter[0, 0], ctf_grid[:, 0], peak_count, peak_orient, peak_row, peak_col,
        forward, back, bins,
    )
    return (
        (top * (1.0 / length)).reshape(1, 1, -1),
        (added * (1.0 / (length * orients * R))).reshape(1, 1, -1),
        (refined * (1.0 / length)).T.reshape(1, listed, defoci),
        best * (1.0 / length),
    )


def merged(x, axis, combine):
    everything = jax.tree.map(
        lambda part, kind: lax.all_gather(part.astype(kind), axis), x, (jnp.bfloat16, jnp.bfloat16)
    )

    def take(k):
        return jax.tree.map(lambda part, own: part[k].astype(own.dtype), everything, x)

    return lax.fori_loop(
        1, lax.axis_size(axis), lambda k, so_far: combine(so_far, take(k)), take(0)
    )


def dft_tables(length):
    steps = jnp.arange(length, dtype=jnp.int32)
    phase = (steps[:, None] * steps[None, :] % length).astype(jnp.float32) * (2.0 * jnp.pi / length)
    cosv = jnp.cos(phase).astype(jnp.bfloat16)
    sinv = jnp.sin(phase).astype(jnp.bfloat16)
    wide = jnp.concatenate([jnp.concatenate([cosv, sinv], 1), jnp.concatenate([-sinv, cosv], 1)], 0)
    back = jnp.stack([cosv, -sinv], axis=1)
    return (wide, back)


def combine_stats(first, second):
    return (jnp.maximum(first[0], second[0]), first[1] + second[1])


def shards(
    interp_index,
    interp_weight,
    volume,
    spectrum,
    ctf_filter,
    peak_count,
    peak_orient,
    peak_row,
    peak_col,
    ctf_grid,
):
    table = volume[:, 0, 0]
    weighted = interpolate(interp_index, interp_weight, table)
    length = spectrum.shape[4]
    half = spectrum.shape[3]
    orients = weighted.shape[1]
    slots = peak_orient.shape[0]
    wide, back = dft_tables(length)
    spec = spectrum[:, 0, 0]
    filt = ctf_filter[0, 0]
    piece = lax.all_gather(weighted, "tile", axis=3, tiled=True)
    count = piece.shape[3]
    spec_rows = spec.astype(jnp.float32)
    filt_rows = filt.astype(jnp.float32)
    sr = piece[0, :, 0].astype(jnp.float32)
    si = piece[1, :, 0].astype(jnp.float32)
    cr = filt_rows * sr
    ci = filt_rows * si
    xr = spec_rows[0] * cr + spec_rows[1] * ci
    xi = spec_rows[1] * cr - spec_rows[0] * ci
    cross = jnp.stack([xr, xi], axis=2).astype(jnp.bfloat16)
    rows_out = jnp.dot(
        cross.reshape(orients * count, 2 * length), wide, preferred_element_type=jnp.float32
    )
    rows_out = rows_out.astype(jnp.bfloat16).reshape(orients, count, 2, length)
    picked_r = jnp.take(sr, peak_orient, axis=0)
    picked_i = jnp.take(si, peak_orient, axis=0)
    plain_r = spec_rows[0] * picked_r + spec_rows[1] * picked_i
    plain_i = spec_rows[1] * picked_r - spec_rows[0] * picked_i
    plain = jnp.stack([plain_r, plain_i], axis=2).astype(jnp.bfloat16)
    combined = jnp.concatenate([rows_out, plain], axis=0)
    halfimg = combined[:orients]
    plain = combined[orients:].astype(jnp.float32)
    offset = lax.axis_index("nar") * half
    back_rows = lax.dynamic_slice_in_dim(back, offset, half, 2)
    partial_value = jnp.einsum(
        "yck,okcx->oyx", back_rows, halfimg, preferred_element_type=jnp.float32
    )
    summed = lax.psum_scatter(
        partial_value.astype(jnp.bfloat16), "nar", scatter_dimension=2, tiled=True
    ).astype(jnp.float32)
    corr = summed * (1.0 / length)
    local_max = jnp.max(corr, axis=0)
    local_sum = jnp.sum(corr, axis=0)
    group_count = lax.axis_size("rot")
    top, total = merged((local_max, local_sum), "rot", combine_stats)
    mean = total / (orients * group_count)
    freq_rows = lax.axis_index("nar") * half + jnp.arange(half, dtype=jnp.int32)
    freq_cols = jnp.arange(length, dtype=jnp.int32)
    unit = 2.0 * jnp.pi / length
    row_turn = ((freq_rows[None, :] * peak_row[:, None]) % length).astype(jnp.float32) * unit
    col_turn = ((freq_cols[None, :] * peak_col[:, None]) % length).astype(jnp.float32) * unit
    rc, rs = jnp.cos(row_turn)[:, :, None], jnp.sin(row_turn)[:, :, None]
    cc, cs = jnp.cos(col_turn)[:, None, :], jnp.sin(col_turn)[:, None, :]
    shifted = plain[:, :, 0] * (rc * cc - rs * cs) - plain[:, :, 1] * (rs * cc + rc * cs)
    binned = jnp.sum(shifted.reshape(slots, half, length // 4, 4), axis=3).astype(jnp.bfloat16)
    valid = jnp.arange(slots, dtype=jnp.int32) < peak_count[0, 0]
    binned = jnp.where(valid[:, None, None], binned, jnp.zeros_like(binned)).reshape(slots, -1)
    grid_local = ctf_grid[:, 0]
    grid_count = grid_local.shape[0]
    listed = lax.axis_size("tile") * slots
    part = lax.dot_general(
        lax.all_gather(binned, "tile", axis=0, tiled=True),
        grid_local,
        (((1,), (1,)), ((), ())),
        preferred_element_type=jnp.float32,
    )
    refined = lax.psum(part, "nar") * (1.0 / length)
    best = lax.pmax(jnp.max(refined, axis=1), "tile")
    return (
        top.reshape(1, 1, -1),
        mean.reshape(1, 1, -1),
        refined.reshape(1, listed, grid_count),
        best.reshape(1, listed),
    )


def fits(sizes, args):
    R, T, N = sizes
    _, orients, _, rows, length = args[0].shape
    half, slots, defoci = args[3].shape[3], args[6].shape[0], args[9].shape[0]
    return (
        rows % PACK == 0
        and orients * rows // PACK % 2 == 0
        and T <= 8
        and T * rows == half
        and N * half == length
        and length % LANES == 0
        and length % (N * R * PACK) == 0
        and defoci == SUBL
        and defoci % R == 0
        and T * slots <= LANES
        and length // 4 <= LANES
        and args[9].shape[2] == half * (length // 4)
        and args[9].shape[2] % (R * length) == 0
    )


def solution(mesh):
    sizes = tuple(mesh.shape[axis] for axis in ("rot", "tile", "nar"))

    def body(*args):
        return fused(sizes, args) if fits(sizes, args) else shards(*args)

    return jax.shard_map(
        body,
        mesh=mesh,
        in_specs=(
            P(None, "rot", "nar", "tile", None),
            P(None, "rot", "nar", "tile", None),
            P(None, "nar", "tile", None),
            P(None, "tile", "nar", None, None),
            P("tile", "nar", None, None),
            P("rot", "tile"),
            P(("rot", "tile")),
            P(("rot", "tile")),
            P(("rot", "tile")),
            P("tile", "nar", None),
        ),
        out_specs=(
            P("tile", "nar", None),
            P("tile", "nar", None),
            P("rot", None, "tile"),
            P("rot", None),
        ),
        check_vma=False,
    )
```

```python
import functools
import math

import jax
import jax.numpy as jnp
import ml_dtypes
import numpy as np
from jax import lax
from jax.experimental import pallas as pl
from jax.experimental.pallas import tpu as pltpu
from jax.sharding import PartitionSpec as P

LANES = 128
SUBL = 8
PACK = 16


def select_tree(items, bits):
    for bit in bits:
        items = [jnp.where(bit, b, a) for a, b in zip(items[::2], items[1::2])]
    return items[0]


def encode(values):
    rest = jnp.abs(values) * 0.125
    exponent = jnp.zeros_like(rest)
    for step in (64, 32, 16, 8, 4, 2, 1):
        small = rest < 2.0**-step
        rest = jnp.where(small, rest * 2.0**step, rest)
        exponent = jnp.where(small, exponent + step, exponent)
    mantissa = jnp.floor(rest * 256.0)
    mantissa = jnp.where(values < 0, -mantissa, mantissa)
    return (mantissa * 128.0 + exponent).astype(jnp.int32)


def decode(code):
    scale = jnp.exp2(-5.0 - (code & 127).astype(jnp.float32))
    return (code >> 7).astype(jnp.float32) * scale


def spread_table(table_ref, spread):
    for h in range(spread.shape[0]):
        code = encode(table_ref[:, h * LANES : (h + 1) * LANES].astype(jnp.float32))
        word = code[0:1] * 65536 + (code[1:2] & 65535)
        spread[h] = jnp.broadcast_to(word, (SUBL, LANES))


def lookup(spread, index):
    rows = spread.shape[0]
    low = index & (LANES - 1)
    high = index >> 7
    bits = [((high >> b) & 1) == 1 for b in range(rows.bit_length() - 1)]
    word = select_tree(
        [
            jnp.take_along_axis(spread[h], low, axis=1, mode="promise_in_bounds")
            for h in range(rows)
        ],
        bits,
    )
    return [decode(word >> 16), decode((word << 16) >> 16)]


def interpolate_block(spread, index_ref, weight_ref, o, r, col):
    parts = []
    weights = [
        weight_ref[k, o, pl.ds(r, PACK), pl.ds(col, LANES)].astype(jnp.float32)
        for k in range(index_ref.shape[0])
    ]
    for s in range(0, PACK, SUBL):
        total = None
        for k in range(index_ref.shape[0]):
            found = lookup(spread, index_ref[k, o, pl.ds(r + s, SUBL), pl.ds(col, LANES)])
            w = weights[k][s : s + SUBL]
            terms = [w * v for v in found]
            total = terms if total is None else [a + b for a, b in zip(total, terms)]
        parts.append(total)
    return [jnp.concatenate([p[c] for p in parts], axis=0) for c in range(2)]


def interpolate_kernel(table_ref, index_ref, weight_ref, out_ref, spread):
    spread_table(table_ref, spread)
    _, orients, rows, columns = index_ref.shape
    per_row = columns // LANES
    blocks = rows // PACK * per_row

    def step(i, carry):
        o, rest = i // blocks, i % blocks
        r = pl.multiple_of(rest // per_row * PACK, PACK)
        col = pl.multiple_of(rest % per_row * LANES, LANES)
        found = interpolate_block(spread, index_ref, weight_ref, o, r, col)
        for c in range(2):
            out_ref[c, o, pl.ds(r, PACK), pl.ds(col, LANES)] = found[c].astype(jnp.bfloat16)
        return carry

    lax.fori_loop(0, orients * blocks, step, 0)


def interpolate(interp_index, interp_weight, table):
    _, orients, _, rows, columns = interp_index.shape
    index, weight = interp_index[:, :, 0], interp_weight[:, :, 0]
    short = -rows % PACK
    if short:
        pad = ((0, 0), (0, 0), (0, short), (0, 0))
        index, weight = jnp.pad(index, pad), jnp.pad(weight, pad)
    vmem = pl.BlockSpec(memory_space=pltpu.VMEM)
    out = pl.pallas_call(
        interpolate_kernel,
        out_shape=jax.ShapeDtypeStruct((2, orients, rows + short, columns), jnp.bfloat16),
        in_specs=[vmem] * 3,
        out_specs=vmem,
        scratch_shapes=[pltpu.VMEM((table.shape[1] // LANES, SUBL, LANES), jnp.int32)],
        compiler_params=pltpu.CompilerParams(vmem_limit_bytes=32 * 2**20),
        name="interpolate",
    )(table, index, weight)
    return out[:, :, None, :rows]


def angle(turns, length):
    turns = turns - length * jnp.floor((turns + 0.5) * (1.0 / length))
    turns = jnp.where(turns > 0.5 * length, turns - length, turns)
    x = turns * (2.0 * math.pi / length)
    square = x * x
    cosine = jnp.full_like(x, 1.0 / math.factorial(18) * -1.0)
    sine = jnp.full_like(x, 1.0 / math.factorial(17))
    for p in range(16, -1, -2):
        cosine = cosine * square + (-1.0) ** (p // 2) / math.factorial(p)
    for p in range(15, 0, -2):
        sine = sine * square + (-1.0) ** (p // 2) / math.factorial(p)
    return cosine, sine * x


def push(source, target, send, receive, where):
    return pltpu.make_async_remote_copy(
        src_ref=source,
        dst_ref=target,
        send_sem=send,
        recv_sem=receive,
        device_id=where,
        device_id_type=pl.DeviceIdType.MESH,
    )


def fused_kernel(
    sizes,
    table_hbm, index_hbm, weight_hbm, spec_hbm, filt_hbm, grid_hbm,
    count_hbm, orient_hbm, row_hbm, col_hbm, forward_hbm, back_hbm, bins_hbm,
    top_ref, added_ref, refined_ref, best_ref,
    table_ref, index_ref, weight_ref, spec_ref, filt_ref, forward, back, bins_ref,
    count_ref, orient_ref, row_ref, col_ref,
    spread, slices, grids, cross, shifted, turn, binned, rows_of, scores,
    sent, held, mine, shared,
    local_sem, slice_send, slice_recv, grid_send, grid_recv, share_send, share_recv,
    half_send, half_recv, map_send, map_recv, score_send, score_recv,
):
    R, T, N = sizes
    r, t, n = lax.axis_index("rot"), lax.axis_index("tile"), lax.axis_index("nar")
    slots = orient_ref.shape[0]
    half, length = filt_ref.shape
    chunks = index_ref.shape[2] // PACK
    orients = index_ref.shape[1]
    blocks = length // LANES
    span = grids.shape[-1]
    f32, bf16 = jnp.float32, jnp.bfloat16

    barrier = pltpu.get_barrier_semaphore()
    across = [(dr, dn) for dn in range(N - 1, -1, -1) for dr in range(R) if dr or dn]
    along = [(dt, dn) for dn in range(N) for dt in range(T) if dt or dn]

    def rot_nar(dr, dn):
        return {"rot": lax.rem(r + dr, R), "tile": t, "nar": lax.rem(n + dn, N)}

    def tile_nar(dt, dn):
        return {"rot": r, "tile": lax.rem(t + dt, T), "nar": lax.rem(n + dn, N)}

    peers = [rot_nar(*d) for d in across] + [tile_nar(*d) for d in along if d[0]]
    for where in peers:
        pl.semaphore_signal(barrier, inc=1, device_id=where, device_id_type=pl.DeviceIdType.MESH)
    quarter = grid_hbm.at[:, pl.ds(pl.multiple_of(r * span, span), span)]
    pairs = dict(
        table=(table_hbm, table_ref),
        spec=(spec_hbm, spec_ref),
        filt=(filt_hbm, filt_ref),
        grid=(quarter, grids.at[r, t]),
        forward=(forward_hbm, forward),
        count=(count_hbm, count_ref),
        orient=(orient_hbm, orient_ref),
        row=(row_hbm, row_ref),
        col=(col_hbm, col_ref),
        bins=(bins_hbm, bins_ref),
        back=(back_hbm, back),
    )
    for o in range(orients):
        pairs[f"index{o}"] = (index_hbm.at[:, o], index_ref.at[:, o])
        pairs[f"weight{o}"] = (weight_hbm.at[:, o], weight_ref.at[:, o])
    first = ["table", "index0", "weight0"]
    order = first + [name for name in pairs if name not in first]
    inputs = {
        name: pltpu.make_async_copy(*pairs[name], local_sem.at[k]) for k, name in enumerate(order)
    }
    for name in order:
        inputs[name].start()
    inputs["table"].wait()
    spread_table(table_ref, spread)
    pl.semaphore_wait(barrier, len(peers))

    def grid_copy(d):
        return push(quarter, grids.at[r, t], grid_send.at[d - 1], grid_recv.at[d - 1], tile_nar(d, 0))

    far = lax.rem(r + 2, R)
    pair = r + 1 - 2 * lax.rem(r, 2)
    share_sent = ((r, far), (r, pair), (far, pair))
    share_found = (far, pair, lax.rem(pair + 2, R))

    def share_copy(k, which, to):
        here = grids.at[which]
        return push(here, here, share_send.at[k], share_recv.at[k], {"rot": to, "tile": t, "nar": n})

    def share_arrived(k):
        share_copy(k, share_found[k], share_sent[k][1]).wait_recv()

    for d in range(1, T):
        grid_copy(d).start()

    def slice_copy(i, d):
        here = slices.at[t, lax.rem(i, chunks), i // chunks]
        return push(here, here, slice_send.at[i, d - 1], slice_recv.at[i, d - 1], tile_nar(d, 0))

    def half_copy(o, dr, dn):
        k = dn * R + dr - 1
        return push(
            sent.at[o, dn, lax.rem(r + dr, R)], held.at[n, r, o],
            half_send.at[o, k], half_recv.at[o, k], rot_nar(dr, dn),
        )

    def products(o):
        def arrived(i, carry):
            for d in range(1, T):
                there = slices.at[lax.rem(t + T - d, T), lax.rem(i, chunks), i // chunks]
                push(there, there, slice_send.at[i, d - 1], slice_recv.at[i, d - 1], tile_nar(d, 0)).wait_recv()
            return carry

        lax.fori_loop(o * chunks, (o + 1) * chunks, arrived, 0)

        def product(place, carry):
            down = pl.ds(pl.multiple_of(place * PACK, PACK), PACK)
            for b in range(blocks):
                lanes = slice(b * LANES, (b + 1) * LANES)
                mr, mi = (spec_ref[c, down, lanes].astype(f32) for c in range(2))
                filt = filt_ref[down, lanes].astype(f32)
                sr, si = (
                    slices[place // chunks, lax.rem(place, chunks), o, c, :, lanes].astype(f32)
                    for c in range(2)
                )
                cr, ci = filt * sr, filt * si
                cross[o, down, lanes] = (mr * cr + mi * ci).astype(bf16)
                cross[o, down, length + b * LANES : length + (b + 1) * LANES] = (
                    mi * cr - mr * ci
                ).astype(bf16)
            return carry

        lax.fori_loop(0, half // PACK, product, 0)
        for dn in range(N - 1, -1, -1):
            full = lax.dot_general(
                forward[lax.rem(n + dn, N)], cross[o], (((1,), (1,)), ((), ())),
                preferred_element_type=f32,
            ).astype(bf16)
            sent[o, dn] = full.reshape(sent.shape[2:])
            for dr in range(R):
                if dr or dn:
                    half_copy(o, dr, dn).start()
        held[n, r, o] = sent[o, 0, r]

    total = orients * chunks

    def form(i, carry):
        o, j = i // chunks, lax.rem(i, chunks)
        for k in range(orients):
            @pl.when(i == k * chunks)
            def _():
                inputs[f"index{k}"].wait()
                inputs[f"weight{k}"].wait()

        @pl.when(i == total - 2)
        def _():
            for d in range(1, T):
                grid_copy(d).wait()
            inputs["grid"].wait()
            for k in range(2):
                share_copy(k, *share_sent[k]).start()

        def block(b, carry):
            col = pl.multiple_of(b * LANES, LANES)
            start = pl.multiple_of(j * PACK, PACK)
            found = interpolate_block(spread, index_ref, weight_ref, o, start, col)
            for c in range(2):
                slices[t, j, o, c, :, pl.ds(col, LANES)] = found[c].astype(bf16)
            return carry

        lax.fori_loop(0, blocks, block, 0)
        for d in range(1, T):
            slice_copy(i, d).start()
        return carry

    lax.fori_loop(0, total, form, 0)

    for name in ("spec", "filt", "forward", "count", "orient", "row", "col", "bins", "back"):
        inputs[name].wait()
    ky = lax.broadcasted_iota(jnp.int32, (half, LANES), 0) + n * half
    kx = lax.broadcasted_iota(jnp.int32, (PACK, length), 1)
    for i in range(slots):
        c, s = angle((ky * row_ref[i]).astype(f32), length)
        rows_of[0, i], rows_of[1, i] = c, s
        c, s = angle((kx * col_ref[i]).astype(f32), length)
        turn[0, i], turn[1, i] = c, s

    for o in range(orients):
        products(o)
    share_arrived(0)
    share_copy(2, *share_sent[2]).start()

    def peaks(place, carry):
        down = pl.ds(pl.multiple_of(place * PACK, PACK), PACK)
        for b in range(blocks):
            lanes = slice(b * LANES, (b + 1) * LANES)
            mr, mi = (spec_ref[c, down, lanes].astype(f32) for c in range(2))
            plain = []
            for o in range(orients):
                sr, si = (
                    slices[place // chunks, lax.rem(place, chunks), o, c, :, lanes].astype(f32)
                    for c in range(2)
                )
                pr, pi = mr * sr + mi * si, mi * sr - mr * si
                plain.append((pr.astype(bf16).astype(f32), pi.astype(bf16).astype(f32)))
            for i in range(slots):
                pr, pi = plain[0]
                for o in range(1, orients):
                    chosen = orient_ref[i] == o
                    pr = jnp.where(chosen, plain[o][0], pr)
                    pi = jnp.where(chosen, plain[o][1], pi)
                cc, cs = turn[0, i, :, lanes], turn[1, i, :, lanes]
                rc, rs = rows_of[0, i, down, :], rows_of[1, i, down, :]
                value = rc * (pr * cc - pi * cs) - rs * (pr * cs + pi * cc)
                shifted[b, pl.ds(pl.multiple_of(i * half + place * PACK, PACK), PACK), :] = value
        return carry

    lax.fori_loop(0, half // PACK, peaks, 0)
    group = half // 4
    flat = jnp.concatenate(
        [
            jnp.concatenate(
                [
                    shifted[b, pl.ds(i * half + v, group, stride=4), :].astype(bf16)
                    for v in range(4)
                    for b in range(blocks)
                ],
                axis=1,
            )
            for i in range(slots)
        ],
        axis=0,
    )
    flat = jnp.dot(flat, bins_ref[...], preferred_element_type=f32)
    for i in range(slots):
        part = flat[i * group : (i + 1) * group].astype(bf16).astype(f32)
        part = jnp.where(count_ref[0, 0] > i, part, jnp.zeros_like(part))
        for b in range(blocks):
            binned[i, b] = part[:, b * LANES : (b + 1) * LANES]

    for k in range(1, 3):
        share_arrived(k)
    for k in range(3):
        share_copy(k, *share_sent[k]).wait_send()
    per = span // length
    defoci = grids.shape[2]

    def assess(m, acc):
        a, within = m // per, lax.rem(m, per)
        for b in range(blocks):
            lanes = pl.ds(pl.multiple_of(within * length + b * LANES, LANES), LANES)
            g = [grids[a, k, :, lanes].astype(f32) for k in range(T)]
            for i in range(slots):
                row = jnp.broadcast_to(
                    binned[i, b, pl.ds(m, 1), :], (defoci, LANES)
                )
                acc = [
                    value + g[k % T] * row if k // T == i else value for k, value in enumerate(acc)
                ]
        return acc

    acc = lax.fori_loop(0, group, assess, [jnp.zeros((defoci, LANES), f32)] * (slots * T))
    lane = lax.broadcasted_iota(jnp.int32, (defoci, LANES), 1)
    for k in range(T):
        mixed = jnp.zeros((defoci, LANES), f32)
        for i in range(slots):
            summed = jnp.sum(acc[i * T + k], axis=1, keepdims=True)
            mixed = jnp.where(lane == t * slots + i, summed, mixed)
        scores[n, t, k * defoci : (k + 1) * defoci, :] = mixed

    def score_copy(k, dt, dn):
        return push(scores.at[n, t], scores.at[n, t], score_send.at[k], score_recv.at[k], tile_nar(dt, dn))

    for k, d in enumerate(along):
        score_copy(k, *d).start()

    rows = held.shape[4]
    parts = []
    for o in range(orients):
        for dr, dn in across:
            there = held.at[lax.rem(n + N - dn, N), lax.rem(r + R - dr, R), o]
            k = dn * R + dr - 1
            push(there, there, half_send.at[o, k], half_recv.at[o, k], rot_nar(dr, dn)).wait_recv()
        corr = None
        for m in range(N):
            for c in range(2):
                part = jnp.dot(
                    held[m, :, o, c].reshape(R * rows, half), back[m, c], preferred_element_type=f32
                )
                corr = part if corr is None else corr + part
        parts += [corr[a * rows : (a + 1) * rows] for a in range(R)]
    top = functools.reduce(jnp.maximum, parts)
    added = functools.reduce(lambda a, b: a + b, parts)
    shared[r, 0], shared[r, 1] = top.astype(bf16), added.astype(bf16)
    map_copies = [
        push(shared.at[r], shared.at[r], map_send.at[d - 1], map_recv.at[d - 1], rot_nar(d, 0))
        for d in range(1, R)
    ]
    for copy in map_copies:
        copy.start()

    for k, (dt, dn) in enumerate(along):
        there = scores.at[lax.rem(n + N - dn, N), lax.rem(t + T - dt, T)]
        push(there, there, score_send.at[k], score_recv.at[k], tile_nar(dt, dn)).wait_recv()
    whole = None
    for b in range(T):
        for m in range(N):
            whole = scores[m, b] if whole is None else whole + scores[m, b]
    mine[...] = whole
    listed = T * slots
    best_ref[...] = jnp.max(whole, axis=0, keepdims=True)[:, :listed]
    refined_ref[...] = mine[pl.ds(pl.multiple_of(t * defoci, defoci), defoci), :][:, :listed]

    def left(i, carry):
        for d in range(1, T):
            slice_copy(i, d).wait_send()
        return carry

    lax.fori_loop(0, total, left, 0)
    for o in range(orients):
        for d in across:
            half_copy(o, *d).wait_send()
    for k, d in enumerate(along):
        score_copy(k, *d).wait_send()
    for d in range(1, R):
        there = shared.at[lax.rem(r + R - d, R)]
        push(there, there, map_send.at[d - 1], map_recv.at[d - 1], rot_nar(d, 0)).wait_recv()
    for k, out_ref in enumerate((top_ref, added_ref)):
        full = jnp.concatenate([shared[a, k].astype(f32) for a in range(R)], axis=0)
        paired = jnp.concatenate([full[:, :half], full[:, half:]], axis=0).T
        for b in range(blocks):
            out_ref[pl.ds(b, half, stride=blocks), :] = paired[:, b * LANES : (b + 1) * LANES]
    for copy in map_copies:
        copy.wait_send()


def constants(length, half, R, N):
    steps = np.arange(length)
    phase = (steps[:, None] * steps[None, :] % length).astype(np.float64) * (2.0 * np.pi / length)
    cosv, sinv = np.cos(phase), np.sin(phase)
    by_x = np.stack([np.concatenate([cosv, -sinv], 0).T, np.concatenate([sinv, cosv], 0).T])
    rows = length // (N * R)
    forward = by_x.reshape(2, N, R, rows, 2 * length).transpose(1, 2, 0, 3, 4)
    forward = forward.reshape(N, R * 2 * rows, 2 * length)
    back = np.stack([cosv, -sinv], 0).reshape(2, N, half, length // 2, 2)
    back = back.transpose(1, 0, 2, 4, 3).reshape(N, 2, half, length)
    bins = np.zeros((4, length, 4, length // 4))
    for v in range(4):
        bins[v, steps, v, steps // 4] = 1.0
    bins = bins.reshape(4 * length, length)
    return [jnp.asarray(a.astype(ml_dtypes.bfloat16)) for a in (forward, back, bins)]


def fused(sizes, args):
    (interp_index, interp_weight, volume, spectrum, ctf_filter, peak_count, peak_orient, peak_row,
     peak_col, ctf_grid) = args
    R, T, N = sizes
    neighbours, orients, _, rows, length = interp_index.shape
    half = spectrum.shape[3]
    slots = peak_orient.shape[0]
    defoci, _, bins_all = ctf_grid.shape
    chunks = rows // PACK
    share = length // (N * R)
    entries = volume.shape[3]
    forward, back, bins = constants(length, half, R, N)
    vmem = pl.BlockSpec(memory_space=pltpu.VMEM)
    hbm = pl.BlockSpec(memory_space=pl.ANY)
    f32, bf16, i32 = jnp.float32, jnp.bfloat16, jnp.int32
    total, peers, near = orients * chunks, R * N - 1, T * N - 1
    listed = T * slots
    dma = pltpu.SemaphoreType.DMA
    flat = length * half // LANES
    top, added, refined, best = pl.pallas_call(
        functools.partial(fused_kernel, sizes),
        out_shape=(
            jax.ShapeDtypeStruct((flat, LANES), f32),
            jax.ShapeDtypeStruct((flat, LANES), f32),
            jax.ShapeDtypeStruct((defoci, listed), f32),
            jax.ShapeDtypeStruct((1, listed), f32),
        ),
        in_specs=[hbm] * 13,
        out_specs=(vmem,) * 4,
        scratch_shapes=[
            pltpu.VMEM((2, entries), bf16),
            pltpu.VMEM((neighbours, orients, rows, length), i32),
            pltpu.VMEM((neighbours, orients, rows, length), bf16),
            pltpu.VMEM((2, half, length), bf16),
            pltpu.VMEM((half, length), bf16),
            pltpu.VMEM(forward.shape, bf16),
            pltpu.VMEM(back.shape, bf16),
            pltpu.VMEM(bins.shape, bf16),
            pltpu.SMEM((1, 1), i32),
            pltpu.SMEM((slots,), i32),
            pltpu.SMEM((slots,), i32),
            pltpu.SMEM((slots,), i32),
            pltpu.VMEM((entries // LANES, SUBL, LANES), i32),
            pltpu.VMEM((T, chunks, orients, 2, PACK, length), bf16),
            pltpu.VMEM((R, T, defoci, bins_all // R), bf16),
            pltpu.VMEM((orients, half, 2 * length), bf16),
            pltpu.VMEM((length // LANES, slots * half, LANES), f32),
            pltpu.VMEM((2, slots, PACK, length), f32),
            pltpu.VMEM((slots, length // LANES, half // 4, LANES), f32),
            pltpu.VMEM((2, slots, half, LANES), f32),
            pltpu.VMEM((N, T, T * defoci, LANES), f32),
            pltpu.VMEM((orients, N, R, 2, share, half), bf16),
            pltpu.VMEM((N, R, orients, 2, share, half), bf16),
            pltpu.VMEM((T * defoci, LANES), f32),
            pltpu.VMEM((R, 2, share, length), bf16),
            dma((11 + 2 * orients,)),
            dma((total, T - 1)), dma((total, T - 1)),
            dma((T - 1,)), dma((T - 1,)),
            dma((3,)), dma((3,)),
            dma((orients, peers)), dma((orients, peers)),
            dma((R - 1,)), dma((R - 1,)),
            dma((near,)), dma((near,)),
        ],
        compiler_params=pltpu.CompilerParams(
            collective_id=0, has_side_effects=True, vmem_limit_bytes=60 * 2**20
        ),
        name="match",
    )(
        volume[:, 0, 0], interp_index[:, :, 0], interp_weight[:, :, 0], spectrum[:, 0, 0],
        ctf_filter[0, 0], ctf_grid[:, 0], peak_count, peak_orient, peak_row, peak_col,
        forward, back, bins,
    )
    return (
        (top * (1.0 / length)).reshape(1, 1, -1),
        (added * (1.0 / (length * orients * R))).reshape(1, 1, -1),
        (refined * (1.0 / length)).T.reshape(1, listed, defoci),
        best * (1.0 / length),
    )


def merged(x, axis, combine):
    everything = jax.tree.map(
        lambda part, kind: lax.all_gather(part.astype(kind), axis), x, (jnp.bfloat16, jnp.bfloat16)
    )

    def take(k):
        return jax.tree.map(lambda part, own: part[k].astype(own.dtype), everything, x)

    return lax.fori_loop(
        1, lax.axis_size(axis), lambda k, so_far: combine(so_far, take(k)), take(0)
    )


def dft_tables(length):
    steps = jnp.arange(length, dtype=jnp.int32)
    phase = (steps[:, None] * steps[None, :] % length).astype(jnp.float32) * (2.0 * jnp.pi / length)
    cosv = jnp.cos(phase).astype(jnp.bfloat16)
    sinv = jnp.sin(phase).astype(jnp.bfloat16)
    wide = jnp.concatenate([jnp.concatenate([cosv, sinv], 1), jnp.concatenate([-sinv, cosv], 1)], 0)
    back = jnp.stack([cosv, -sinv], axis=1)
    return (wide, back)


def combine_stats(first, second):
    return (jnp.maximum(first[0], second[0]), first[1] + second[1])


def shards(
    interp_index,
    interp_weight,
    volume,
    spectrum,
    ctf_filter,
    peak_count,
    peak_orient,
    peak_row,
    peak_col,
    ctf_grid,
):
    table = volume[:, 0, 0]
    weighted = interpolate(interp_index, interp_weight, table)
    length = spectrum.shape[4]
    half = spectrum.shape[3]
    orients = weighted.shape[1]
    slots = peak_orient.shape[0]
    wide, back = dft_tables(length)
    spec = spectrum[:, 0, 0]
    filt = ctf_filter[0, 0]
    piece = lax.all_gather(weighted, "tile", axis=3, tiled=True)
    count = piece.shape[3]
    spec_rows = spec.astype(jnp.float32)
    filt_rows = filt.astype(jnp.float32)
    sr = piece[0, :, 0].astype(jnp.float32)
    si = piece[1, :, 0].astype(jnp.float32)
    cr = filt_rows * sr
    ci = filt_rows * si
    xr = spec_rows[0] * cr + spec_rows[1] * ci
    xi = spec_rows[1] * cr - spec_rows[0] * ci
    cross = jnp.stack([xr, xi], axis=2).astype(jnp.bfloat16)
    rows_out = jnp.dot(
        cross.reshape(orients * count, 2 * length), wide, preferred_element_type=jnp.float32
    )
    rows_out = rows_out.astype(jnp.bfloat16).reshape(orients, count, 2, length)
    picked_r = jnp.take(sr, peak_orient, axis=0)
    picked_i = jnp.take(si, peak_orient, axis=0)
    plain_r = spec_rows[0] * picked_r + spec_rows[1] * picked_i
    plain_i = spec_rows[1] * picked_r - spec_rows[0] * picked_i
    plain = jnp.stack([plain_r, plain_i], axis=2).astype(jnp.bfloat16)
    combined = jnp.concatenate([rows_out, plain], axis=0)
    halfimg = combined[:orients]
    plain = combined[orients:].astype(jnp.float32)
    offset = lax.axis_index("nar") * half
    back_rows = lax.dynamic_slice_in_dim(back, offset, half, 2)
    partial_value = jnp.einsum(
        "yck,okcx->oyx", back_rows, halfimg, preferred_element_type=jnp.float32
    )
    summed = lax.psum_scatter(
        partial_value.astype(jnp.bfloat16), "nar", scatter_dimension=2, tiled=True
    ).astype(jnp.float32)
    corr = summed * (1.0 / length)
    local_max = jnp.max(corr, axis=0)
    local_sum = jnp.sum(corr, axis=0)
    group_count = lax.axis_size("rot")
    top, total = merged((local_max, local_sum), "rot", combine_stats)
    mean = total / (orients * group_count)
    freq_rows = lax.axis_index("nar") * half + jnp.arange(half, dtype=jnp.int32)
    freq_cols = jnp.arange(length, dtype=jnp.int32)
    unit = 2.0 * jnp.pi / length
    row_turn = ((freq_rows[None, :] * peak_row[:, None]) % length).astype(jnp.float32) * unit
    col_turn = ((freq_cols[None, :] * peak_col[:, None]) % length).astype(jnp.float32) * unit
    rc, rs = jnp.cos(row_turn)[:, :, None], jnp.sin(row_turn)[:, :, None]
    cc, cs = jnp.cos(col_turn)[:, None, :], jnp.sin(col_turn)[:, None, :]
    shifted = plain[:, :, 0] * (rc * cc - rs * cs) - plain[:, :, 1] * (rs * cc + rc * cs)
    binned = jnp.sum(shifted.reshape(slots, half, length // 4, 4), axis=3).astype(jnp.bfloat16)
    valid = jnp.arange(slots, dtype=jnp.int32) < peak_count[0, 0]
    binned = jnp.where(valid[:, None, None], binned, jnp.zeros_like(binned)).reshape(slots, -1)
    grid_local = ctf_grid[:, 0]
    grid_count = grid_local.shape[0]
    listed = lax.axis_size("tile") * slots
    part = lax.dot_general(
        lax.all_gather(binned, "tile", axis=0, tiled=True),
        grid_local,
        (((1,), (1,)), ((), ())),
        preferred_element_type=jnp.float32,
    )
    refined = lax.psum(part, "nar") * (1.0 / length)
    best = lax.pmax(jnp.max(refined, axis=1), "tile")
    return (
        top.reshape(1, 1, -1),
        mean.reshape(1, 1, -1),
        refined.reshape(1, listed, grid_count),
        best.reshape(1, listed),
    )


def fits(sizes, args):
    R, T, N = sizes
    _, orients, _, rows, length = args[0].shape
    half, slots, defoci = args[3].shape[3], args[6].shape[0], args[9].shape[0]
    return (
        rows % PACK == 0
        and orients * rows // PACK % 2 == 0
        and T <= 8
        and R == 4
        and T * rows == half
        and N * half == length
        and length % LANES == 0
        and length % (N * R * PACK) == 0
        and defoci == SUBL
        and defoci % R == 0
        and T * slots <= LANES
        and length // 4 <= LANES
        and args[9].shape[2] == half * (length // 4)
        and args[9].shape[2] % (R * length) == 0
    )


def solution(mesh):
    sizes = tuple(mesh.shape[axis] for axis in ("rot", "tile", "nar"))

    def body(*args):
        return fused(sizes, args) if fits(sizes, args) else shards(*args)

    return jax.shard_map(
        body,
        mesh=mesh,
        in_specs=(
            P(None, "rot", "nar", "tile", None),
            P(None, "rot", "nar", "tile", None),
            P(None, "nar", "tile", None),
            P(None, "tile", "nar", None, None),
            P("tile", "nar", None, None),
            P("rot", "tile"),
            P(("rot", "tile")),
            P(("rot", "tile")),
            P(("rot", "tile")),
            P("tile", "nar", None),
        ),
        out_specs=(
            P("tile", "nar", None),
            P("tile", "nar", None),
            P("rot", None, "tile"),
            P("rot", None),
        ),
        check_vma=False,
    )
```

```python
import functools
import math

import jax
import jax.numpy as jnp
import ml_dtypes
import numpy as np
from jax import lax
from jax.experimental import pallas as pl
from jax.experimental.pallas import tpu as pltpu
from jax.sharding import PartitionSpec as P

LANES = 128
SUBL = 8
PACK = 16


def select_tree(items, bits):
    for bit in bits:
        items = [jnp.where(bit, b, a) for a, b in zip(items[::2], items[1::2])]
    return items[0]


def encode(values):
    rest = jnp.abs(values) * 0.125
    exponent = jnp.zeros_like(rest)
    for step in (64, 32, 16, 8, 4, 2, 1):
        small = rest < 2.0**-step
        rest = jnp.where(small, rest * 2.0**step, rest)
        exponent = jnp.where(small, exponent + step, exponent)
    mantissa = jnp.floor(rest * 256.0)
    mantissa = jnp.where(values < 0, -mantissa, mantissa)
    return (mantissa * 128.0 + exponent).astype(jnp.int32)


def decode(code):
    scale = jnp.exp2(-5.0 - (code & 127).astype(jnp.float32))
    return (code >> 7).astype(jnp.float32) * scale


def spread_table(table_ref, spread):
    for h in range(spread.shape[0]):
        code = encode(table_ref[:, h * LANES : (h + 1) * LANES].astype(jnp.float32))
        word = code[0:1] * 65536 + (code[1:2] & 65535)
        spread[h] = jnp.broadcast_to(word, (SUBL, LANES))


def lookup(spread, index):
    rows = spread.shape[0]
    low = index & (LANES - 1)
    high = index >> 7
    bits = [((high >> b) & 1) == 1 for b in range(rows.bit_length() - 1)]
    word = select_tree(
        [
            jnp.take_along_axis(spread[h], low, axis=1, mode="promise_in_bounds")
            for h in range(rows)
        ],
        bits,
    )
    return [decode(word >> 16), decode((word << 16) >> 16)]


def interpolate_block(spread, index_ref, weight_ref, o, r, col):
    parts = []
    weights = [
        weight_ref[k, o, pl.ds(r, PACK), pl.ds(col, LANES)].astype(jnp.float32)
        for k in range(index_ref.shape[0])
    ]
    for s in range(0, PACK, SUBL):
        total = None
        for k in range(index_ref.shape[0]):
            found = lookup(spread, index_ref[k, o, pl.ds(r + s, SUBL), pl.ds(col, LANES)])
            w = weights[k][s : s + SUBL]
            terms = [w * v for v in found]
            total = terms if total is None else [a + b for a, b in zip(total, terms)]
        parts.append(total)
    return [jnp.concatenate([p[c] for p in parts], axis=0) for c in range(2)]


def interpolate_kernel(table_ref, index_ref, weight_ref, out_ref, spread):
    spread_table(table_ref, spread)
    _, orients, rows, columns = index_ref.shape
    per_row = columns // LANES
    blocks = rows // PACK * per_row

    def step(i, carry):
        o, rest = i // blocks, i % blocks
        r = pl.multiple_of(rest // per_row * PACK, PACK)
        col = pl.multiple_of(rest % per_row * LANES, LANES)
        found = interpolate_block(spread, index_ref, weight_ref, o, r, col)
        for c in range(2):
            out_ref[c, o, pl.ds(r, PACK), pl.ds(col, LANES)] = found[c].astype(jnp.bfloat16)
        return carry

    lax.fori_loop(0, orients * blocks, step, 0)


def interpolate(interp_index, interp_weight, table):
    _, orients, _, rows, columns = interp_index.shape
    index, weight = interp_index[:, :, 0], interp_weight[:, :, 0]
    short = -rows % PACK
    if short:
        pad = ((0, 0), (0, 0), (0, short), (0, 0))
        index, weight = jnp.pad(index, pad), jnp.pad(weight, pad)
    vmem = pl.BlockSpec(memory_space=pltpu.VMEM)
    out = pl.pallas_call(
        interpolate_kernel,
        out_shape=jax.ShapeDtypeStruct((2, orients, rows + short, columns), jnp.bfloat16),
        in_specs=[vmem] * 3,
        out_specs=vmem,
        scratch_shapes=[pltpu.VMEM((table.shape[1] // LANES, SUBL, LANES), jnp.int32)],
        compiler_params=pltpu.CompilerParams(vmem_limit_bytes=32 * 2**20),
        name="interpolate",
    )(table, index, weight)
    return out[:, :, None, :rows]


def angle(turns, length):
    turns = turns - length * jnp.floor((turns + 0.5) * (1.0 / length))
    turns = jnp.where(turns > 0.5 * length, turns - length, turns)
    x = turns * (2.0 * math.pi / length)
    square = x * x
    cosine = jnp.full_like(x, 1.0 / math.factorial(18) * -1.0)
    sine = jnp.full_like(x, 1.0 / math.factorial(17))
    for p in range(16, -1, -2):
        cosine = cosine * square + (-1.0) ** (p // 2) / math.factorial(p)
    for p in range(15, 0, -2):
        sine = sine * square + (-1.0) ** (p // 2) / math.factorial(p)
    return cosine, sine * x


def push(source, target, send, receive, where):
    return pltpu.make_async_remote_copy(
        src_ref=source,
        dst_ref=target,
        send_sem=send,
        recv_sem=receive,
        device_id=where,
        device_id_type=pl.DeviceIdType.MESH,
    )


def fused_kernel(
    sizes,
    table_hbm, index_hbm, weight_hbm, spec_hbm, filt_hbm, grid_hbm,
    count_hbm, orient_hbm, row_hbm, col_hbm, forward_hbm, back_hbm, bins_hbm,
    top_ref, added_ref, refined_ref, best_ref,
    table_ref, index_ref, weight_ref, spec_ref, filt_ref, forward, back, bins_ref,
    count_ref, orient_ref, row_ref, col_ref,
    spread, slices, grids, cross, shifted, turn, binned, rows_of, scores,
    sent, held, mine, shared,
    local_sem, slice_send, slice_recv, grid_send, grid_recv, share_send, share_recv,
    half_send, half_recv, map_send, map_recv, score_send, score_recv,
):
    R, T, N = sizes
    r, t, n = lax.axis_index("rot"), lax.axis_index("tile"), lax.axis_index("nar")
    slots = orient_ref.shape[0]
    half, length = filt_ref.shape
    chunks = index_ref.shape[2] // PACK
    orients = index_ref.shape[1]
    blocks = length // LANES
    span = grids.shape[-1]
    f32, bf16 = jnp.float32, jnp.bfloat16

    barrier = pltpu.get_barrier_semaphore()
    across = [(dr, dn) for dn in range(N - 1, -1, -1) for dr in range(R) if dr or dn]
    along = [(dt, dn) for dn in range(N) for dt in range(T) if dt or dn]

    def rot_nar(dr, dn):
        return {"rot": lax.rem(r + dr, R), "tile": t, "nar": lax.rem(n + dn, N)}

    def tile_nar(dt, dn):
        return {"rot": r, "tile": lax.rem(t + dt, T), "nar": lax.rem(n + dn, N)}

    peers = [rot_nar(*d) for d in across] + [tile_nar(*d) for d in along if d[0]]
    for where in peers:
        pl.semaphore_signal(barrier, inc=1, device_id=where, device_id_type=pl.DeviceIdType.MESH)
    quarter = grid_hbm.at[:, pl.ds(pl.multiple_of(r * span, span), span)]
    pairs = dict(
        table=(table_hbm, table_ref),
        spec=(spec_hbm, spec_ref),
        filt=(filt_hbm, filt_ref),
        grid=(quarter, grids.at[r, t]),
        forward=(forward_hbm, forward),
        count=(count_hbm, count_ref),
        orient=(orient_hbm, orient_ref),
        row=(row_hbm, row_ref),
        col=(col_hbm, col_ref),
        bins=(bins_hbm, bins_ref),
        back=(back_hbm, back),
    )
    for o in range(orients):
        pairs[f"index{o}"] = (index_hbm.at[:, o], index_ref.at[:, o])
        pairs[f"weight{o}"] = (weight_hbm.at[:, o], weight_ref.at[:, o])
    first = ["table", "index0", "weight0"]
    order = first + [name for name in pairs if name not in first]
    inputs = {
        name: pltpu.make_async_copy(*pairs[name], local_sem.at[k]) for k, name in enumerate(order)
    }
    for name in order:
        inputs[name].start()
    inputs["table"].wait()
    spread_table(table_ref, spread)
    pl.semaphore_wait(barrier, len(peers))

    def grid_copy(d):
        return push(quarter, grids.at[r, t], grid_send.at[d - 1], grid_recv.at[d - 1], tile_nar(d, 0))

    far = lax.rem(r + 2, R)
    pair = r + 1 - 2 * lax.rem(r, 2)
    share_sent = ((r, far), (r, pair), (far, pair))
    share_found = (far, pair, lax.rem(pair + 2, R))

    def share_copy(k, which, to):
        here = grids.at[which]
        return push(here, here, share_send.at[k], share_recv.at[k], {"rot": to, "tile": t, "nar": n})

    def share_arrived(k):
        share_copy(k, share_found[k], share_sent[k][1]).wait_recv()

    for d in range(1, T):
        grid_copy(d).start()

    def slice_copy(i, d):
        here = slices.at[t, lax.rem(i, chunks), i // chunks]
        return push(here, here, slice_send.at[i, d - 1], slice_recv.at[i, d - 1], tile_nar(d, 0))

    def half_copy(o, dr, dn):
        k = dn * R + dr - 1
        return push(
            sent.at[o, dn, lax.rem(r + dr, R)], held.at[n, r, o],
            half_send.at[o, k], half_recv.at[o, k], rot_nar(dr, dn),
        )

    def products(o):
        def arrived(i, carry):
            for d in range(1, T):
                there = slices.at[lax.rem(t + T - d, T), lax.rem(i, chunks), i // chunks]
                push(there, there, slice_send.at[i, d - 1], slice_recv.at[i, d - 1], tile_nar(d, 0)).wait_recv()
            return carry

        lax.fori_loop(o * chunks, (o + 1) * chunks, arrived, 0)

        def product(place, carry):
            down = pl.ds(pl.multiple_of(place * PACK, PACK), PACK)
            for b in range(blocks):
                lanes = slice(b * LANES, (b + 1) * LANES)
                mr, mi = (spec_ref[c, down, lanes].astype(f32) for c in range(2))
                filt = filt_ref[down, lanes].astype(f32)
                sr, si = (
                    slices[place // chunks, lax.rem(place, chunks), o, c, :, lanes].astype(f32)
                    for c in range(2)
                )
                cr, ci = filt * sr, filt * si
                cross[o, down, lanes] = (mr * cr + mi * ci).astype(bf16)
                cross[o, down, length + b * LANES : length + (b + 1) * LANES] = (
                    mi * cr - mr * ci
                ).astype(bf16)
            return carry

        lax.fori_loop(0, half // PACK, product, 0)
        for dn in range(N - 1, -1, -1):
            full = lax.dot_general(
                forward[lax.rem(n + dn, N)], cross[o], (((1,), (1,)), ((), ())),
                preferred_element_type=f32,
            ).astype(bf16)
            sent[o, dn] = full.reshape(sent.shape[2:])
            for dr in range(R):
                if dr or dn:
                    half_copy(o, dr, dn).start()
        held[n, r, o] = sent[o, 0, r]

    total = orients * chunks

    def form(i, carry):
        o, j = i // chunks, lax.rem(i, chunks)
        for k in range(orients):
            @pl.when(i == k * chunks)
            def _():
                inputs[f"index{k}"].wait()
                inputs[f"weight{k}"].wait()

        @pl.when(i == total - 2)
        def _():
            for d in range(1, T):
                grid_copy(d).wait()
            inputs["grid"].wait()
            for k in range(2):
                share_copy(k, *share_sent[k]).start()

        def block(b, carry):
            col = pl.multiple_of(b * LANES, LANES)
            start = pl.multiple_of(j * PACK, PACK)
            found = interpolate_block(spread, index_ref, weight_ref, o, start, col)
            for c in range(2):
                slices[t, j, o, c, :, pl.ds(col, LANES)] = found[c].astype(bf16)
            return carry

        lax.fori_loop(0, blocks, block, 0)
        for d in range(1, T):
            slice_copy(i, d).start()
        return carry

    lax.fori_loop(0, total, form, 0)

    for name in ("spec", "filt", "forward", "count", "orient", "row", "col", "bins", "back"):
        inputs[name].wait()
    ky = lax.broadcasted_iota(jnp.int32, (half, LANES), 0) + n * half
    kx = lax.broadcasted_iota(jnp.int32, (PACK, length), 1)
    for i in range(slots):
        c, s = angle((ky * row_ref[i]).astype(f32), length)
        rows_of[0, i], rows_of[1, i] = c, s
        c, s = angle((kx * col_ref[i]).astype(f32), length)
        turn[0, i], turn[1, i] = c, s

    for o in range(orients):
        products(o)
    share_arrived(0)
    share_copy(2, *share_sent[2]).start()

    def peaks(place, carry):
        down = pl.ds(pl.multiple_of(place * PACK, PACK), PACK)
        for b in range(blocks):
            lanes = slice(b * LANES, (b + 1) * LANES)
            mr, mi = (spec_ref[c, down, lanes].astype(f32) for c in range(2))
            plain = []
            for o in range(orients):
                sr, si = (
                    slices[place // chunks, lax.rem(place, chunks), o, c, :, lanes].astype(f32)
                    for c in range(2)
                )
                pr, pi = mr * sr + mi * si, mi * sr - mr * si
                plain.append((pr.astype(bf16).astype(f32), pi.astype(bf16).astype(f32)))
            for i in range(slots):
                pr, pi = plain[0]
                for o in range(1, orients):
                    chosen = orient_ref[i] == o
                    pr = jnp.where(chosen, plain[o][0], pr)
                    pi = jnp.where(chosen, plain[o][1], pi)
                cc, cs = turn[0, i, :, lanes], turn[1, i, :, lanes]
                rc, rs = rows_of[0, i, down, :], rows_of[1, i, down, :]
                value = rc * (pr * cc - pi * cs) - rs * (pr * cs + pi * cc)
                shifted[b, pl.ds(pl.multiple_of(i * half + place * PACK, PACK), PACK), :] = value
        return carry

    lax.fori_loop(0, half // PACK, peaks, 0)
    group = half // 4
    flat = jnp.concatenate(
        [
            jnp.concatenate(
                [
                    shifted[b, pl.ds(i * half + v, group, stride=4), :].astype(bf16)
                    for v in range(4)
                    for b in range(blocks)
                ],
                axis=1,
            )
            for i in range(slots)
        ],
        axis=0,
    )
    flat = jnp.dot(flat, bins_ref[...], preferred_element_type=f32)
    for i in range(slots):
        part = flat[i * group : (i + 1) * group].astype(bf16).astype(f32)
        part = jnp.where(count_ref[0, 0] > i, part, jnp.zeros_like(part))
        for b in range(blocks):
            binned[i, b] = part[:, b * LANES : (b + 1) * LANES]

    rows = held.shape[4]
    parts = []
    for o in range(orients):
        for dr, dn in across:
            there = held.at[lax.rem(n + N - dn, N), lax.rem(r + R - dr, R), o]
            k = dn * R + dr - 1
            push(there, there, half_send.at[o, k], half_recv.at[o, k], rot_nar(dr, dn)).wait_recv()
        corr = None
        for m in range(N):
            for c in range(2):
                part = jnp.dot(
                    held[m, :, o, c].reshape(R * rows, half), back[m, c], preferred_element_type=f32
                )
                corr = part if corr is None else corr + part
        parts += [corr[a * rows : (a + 1) * rows] for a in range(R)]
    top = functools.reduce(jnp.maximum, parts)
    added = functools.reduce(lambda a, b: a + b, parts)
    shared[r, 0], shared[r, 1] = top.astype(bf16), added.astype(bf16)
    map_copies = [
        push(shared.at[r], shared.at[r], map_send.at[d - 1], map_recv.at[d - 1], rot_nar(d, 0))
        for d in range(1, R)
    ]
    for copy in map_copies:
        copy.start()

    for k in range(1, 3):
        share_arrived(k)
    for k in range(3):
        share_copy(k, *share_sent[k]).wait_send()
    per = span // length
    defoci = grids.shape[2]

    def assess(m, acc):
        a, within = m // per, lax.rem(m, per)
        for b in range(blocks):
            lanes = pl.ds(pl.multiple_of(within * length + b * LANES, LANES), LANES)
            g = [grids[a, k, :, lanes].astype(f32) for k in range(T)]
            for i in range(slots):
                row = jnp.broadcast_to(
                    binned[i, b, pl.ds(m, 1), :], (defoci, LANES)
                )
                acc = [
                    value + g[k % T] * row if k // T == i else value for k, value in enumerate(acc)
                ]
        return acc

    acc = lax.fori_loop(0, group, assess, [jnp.zeros((defoci, LANES), f32)] * (slots * T))
    lane = lax.broadcasted_iota(jnp.int32, (defoci, LANES), 1)
    for k in range(T):
        mixed = jnp.zeros((defoci, LANES), f32)
        for i in range(slots):
            summed = jnp.sum(acc[i * T + k], axis=1, keepdims=True)
            mixed = jnp.where(lane == t * slots + i, summed, mixed)
        scores[n, t, k * defoci : (k + 1) * defoci, :] = mixed

    def score_copy(k, dt, dn):
        return push(scores.at[n, t], scores.at[n, t], score_send.at[k], score_recv.at[k], tile_nar(dt, dn))

    for k, d in enumerate(along):
        score_copy(k, *d).start()

    for k, (dt, dn) in enumerate(along):
        there = scores.at[lax.rem(n + N - dn, N), lax.rem(t + T - dt, T)]
        push(there, there, score_send.at[k], score_recv.at[k], tile_nar(dt, dn)).wait_recv()
    whole = None
    for b in range(T):
        for m in range(N):
            whole = scores[m, b] if whole is None else whole + scores[m, b]
    mine[...] = whole
    listed = T * slots
    best_ref[...] = jnp.max(whole, axis=0, keepdims=True)[:, :listed]
    refined_ref[...] = mine[pl.ds(pl.multiple_of(t * defoci, defoci), defoci), :][:, :listed]

    def left(i, carry):
        for d in range(1, T):
            slice_copy(i, d).wait_send()
        return carry

    lax.fori_loop(0, total, left, 0)
    for o in range(orients):
        for d in across:
            half_copy(o, *d).wait_send()
    for k, d in enumerate(along):
        score_copy(k, *d).wait_send()
    for d in range(1, R):
        there = shared.at[lax.rem(r + R - d, R)]
        push(there, there, map_send.at[d - 1], map_recv.at[d - 1], rot_nar(d, 0)).wait_recv()
    for k, out_ref in enumerate((top_ref, added_ref)):
        full = jnp.concatenate([shared[a, k].astype(f32) for a in range(R)], axis=0)
        paired = jnp.concatenate([full[:, :half], full[:, half:]], axis=0).T
        for b in range(blocks):
            out_ref[pl.ds(b, half, stride=blocks), :] = paired[:, b * LANES : (b + 1) * LANES]
    for copy in map_copies:
        copy.wait_send()


def constants(length, half, R, N):
    steps = np.arange(length)
    phase = (steps[:, None] * steps[None, :] % length).astype(np.float64) * (2.0 * np.pi / length)
    cosv, sinv = np.cos(phase), np.sin(phase)
    by_x = np.stack([np.concatenate([cosv, -sinv], 0).T, np.concatenate([sinv, cosv], 0).T])
    rows = length // (N * R)
    forward = by_x.reshape(2, N, R, rows, 2 * length).transpose(1, 2, 0, 3, 4)
    forward = forward.reshape(N, R * 2 * rows, 2 * length)
    back = np.stack([cosv, -sinv], 0).reshape(2, N, half, length // 2, 2)
    back = back.transpose(1, 0, 2, 4, 3).reshape(N, 2, half, length)
    bins = np.zeros((4, length, 4, length // 4))
    for v in range(4):
        bins[v, steps, v, steps // 4] = 1.0
    bins = bins.reshape(4 * length, length)
    return [jnp.asarray(a.astype(ml_dtypes.bfloat16)) for a in (forward, back, bins)]


def fused(sizes, args):
    (interp_index, interp_weight, volume, spectrum, ctf_filter, peak_count, peak_orient, peak_row,
     peak_col, ctf_grid) = args
    R, T, N = sizes
    neighbours, orients, _, rows, length = interp_index.shape
    half = spectrum.shape[3]
    slots = peak_orient.shape[0]
    defoci, _, bins_all = ctf_grid.shape
    chunks = rows // PACK
    share = length // (N * R)
    entries = volume.shape[3]
    forward, back, bins = constants(length, half, R, N)
    vmem = pl.BlockSpec(memory_space=pltpu.VMEM)
    hbm = pl.BlockSpec(memory_space=pl.ANY)
    f32, bf16, i32 = jnp.float32, jnp.bfloat16, jnp.int32
    total, peers, near = orients * chunks, R * N - 1, T * N - 1
    listed = T * slots
    dma = pltpu.SemaphoreType.DMA
    flat = length * half // LANES
    top, added, refined, best = pl.pallas_call(
        functools.partial(fused_kernel, sizes),
        out_shape=(
            jax.ShapeDtypeStruct((flat, LANES), f32),
            jax.ShapeDtypeStruct((flat, LANES), f32),
            jax.ShapeDtypeStruct((defoci, listed), f32),
            jax.ShapeDtypeStruct((1, listed), f32),
        ),
        in_specs=[hbm] * 13,
        out_specs=(vmem,) * 4,
        scratch_shapes=[
            pltpu.VMEM((2, entries), bf16),
            pltpu.VMEM((neighbours, orients, rows, length), i32),
            pltpu.VMEM((neighbours, orients, rows, length), bf16),
            pltpu.VMEM((2, half, length), bf16),
            pltpu.VMEM((half, length), bf16),
            pltpu.VMEM(forward.shape, bf16),
            pltpu.VMEM(back.shape, bf16),
            pltpu.VMEM(bins.shape, bf16),
            pltpu.SMEM((1, 1), i32),
            pltpu.SMEM((slots,), i32),
            pltpu.SMEM((slots,), i32),
            pltpu.SMEM((slots,), i32),
            pltpu.VMEM((entries // LANES, SUBL, LANES), i32),
            pltpu.VMEM((T, chunks, orients, 2, PACK, length), bf16),
            pltpu.VMEM((R, T, defoci, bins_all // R), bf16),
            pltpu.VMEM((orients, half, 2 * length), bf16),
            pltpu.VMEM((length // LANES, slots * half, LANES), f32),
            pltpu.VMEM((2, slots, PACK, length), f32),
            pltpu.VMEM((slots, length // LANES, half // 4, LANES), f32),
            pltpu.VMEM((2, slots, half, LANES), f32),
            pltpu.VMEM((N, T, T * defoci, LANES), f32),
            pltpu.VMEM((orients, N, R, 2, share, half), bf16),
            pltpu.VMEM((N, R, orients, 2, share, half), bf16),
            pltpu.VMEM((T * defoci, LANES), f32),
            pltpu.VMEM((R, 2, share, length), bf16),
            dma((11 + 2 * orients,)),
            dma((total, T - 1)), dma((total, T - 1)),
            dma((T - 1,)), dma((T - 1,)),
            dma((3,)), dma((3,)),
            dma((orients, peers)), dma((orients, peers)),
            dma((R - 1,)), dma((R - 1,)),
            dma((near,)), dma((near,)),
        ],
        compiler_params=pltpu.CompilerParams(
            collective_id=0, has_side_effects=True, vmem_limit_bytes=60 * 2**20
        ),
        name="match",
    )(
        volume[:, 0, 0], interp_index[:, :, 0], interp_weight[:, :, 0], spectrum[:, 0, 0],
        ctf_filter[0, 0], ctf_grid[:, 0], peak_count, peak_orient, peak_row, peak_col,
        forward, back, bins,
    )
    return (
        (top * (1.0 / length)).reshape(1, 1, -1),
        (added * (1.0 / (length * orients * R))).reshape(1, 1, -1),
        (refined * (1.0 / length)).T.reshape(1, listed, defoci),
        best * (1.0 / length),
    )


def merged(x, axis, combine):
    everything = jax.tree.map(
        lambda part, kind: lax.all_gather(part.astype(kind), axis), x, (jnp.bfloat16, jnp.bfloat16)
    )

    def take(k):
        return jax.tree.map(lambda part, own: part[k].astype(own.dtype), everything, x)

    return lax.fori_loop(
        1, lax.axis_size(axis), lambda k, so_far: combine(so_far, take(k)), take(0)
    )


def dft_tables(length):
    steps = jnp.arange(length, dtype=jnp.int32)
    phase = (steps[:, None] * steps[None, :] % length).astype(jnp.float32) * (2.0 * jnp.pi / length)
    cosv = jnp.cos(phase).astype(jnp.bfloat16)
    sinv = jnp.sin(phase).astype(jnp.bfloat16)
    wide = jnp.concatenate([jnp.concatenate([cosv, sinv], 1), jnp.concatenate([-sinv, cosv], 1)], 0)
    back = jnp.stack([cosv, -sinv], axis=1)
    return (wide, back)


def combine_stats(first, second):
    return (jnp.maximum(first[0], second[0]), first[1] + second[1])


def shards(
    interp_index,
    interp_weight,
    volume,
    spectrum,
    ctf_filter,
    peak_count,
    peak_orient,
    peak_row,
    peak_col,
    ctf_grid,
):
    table = volume[:, 0, 0]
    weighted = interpolate(interp_index, interp_weight, table)
    length = spectrum.shape[4]
    half = spectrum.shape[3]
    orients = weighted.shape[1]
    slots = peak_orient.shape[0]
    wide, back = dft_tables(length)
    spec = spectrum[:, 0, 0]
    filt = ctf_filter[0, 0]
    piece = lax.all_gather(weighted, "tile", axis=3, tiled=True)
    count = piece.shape[3]
    spec_rows = spec.astype(jnp.float32)
    filt_rows = filt.astype(jnp.float32)
    sr = piece[0, :, 0].astype(jnp.float32)
    si = piece[1, :, 0].astype(jnp.float32)
    cr = filt_rows * sr
    ci = filt_rows * si
    xr = spec_rows[0] * cr + spec_rows[1] * ci
    xi = spec_rows[1] * cr - spec_rows[0] * ci
    cross = jnp.stack([xr, xi], axis=2).astype(jnp.bfloat16)
    rows_out = jnp.dot(
        cross.reshape(orients * count, 2 * length), wide, preferred_element_type=jnp.float32
    )
    rows_out = rows_out.astype(jnp.bfloat16).reshape(orients, count, 2, length)
    picked_r = jnp.take(sr, peak_orient, axis=0)
    picked_i = jnp.take(si, peak_orient, axis=0)
    plain_r = spec_rows[0] * picked_r + spec_rows[1] * picked_i
    plain_i = spec_rows[1] * picked_r - spec_rows[0] * picked_i
    plain = jnp.stack([plain_r, plain_i], axis=2).astype(jnp.bfloat16)
    combined = jnp.concatenate([rows_out, plain], axis=0)
    halfimg = combined[:orients]
    plain = combined[orients:].astype(jnp.float32)
    offset = lax.axis_index("nar") * half
    back_rows = lax.dynamic_slice_in_dim(back, offset, half, 2)
    partial_value = jnp.einsum(
        "yck,okcx->oyx", back_rows, halfimg, preferred_element_type=jnp.float32
    )
    summed = lax.psum_scatter(
        partial_value.astype(jnp.bfloat16), "nar", scatter_dimension=2, tiled=True
    ).astype(jnp.float32)
    corr = summed * (1.0 / length)
    local_max = jnp.max(corr, axis=0)
    local_sum = jnp.sum(corr, axis=0)
    group_count = lax.axis_size("rot")
    top, total = merged((local_max, local_sum), "rot", combine_stats)
    mean = total / (orients * group_count)
    freq_rows = lax.axis_index("nar") * half + jnp.arange(half, dtype=jnp.int32)
    freq_cols = jnp.arange(length, dtype=jnp.int32)
    unit = 2.0 * jnp.pi / length
    row_turn = ((freq_rows[None, :] * peak_row[:, None]) % length).astype(jnp.float32) * unit
    col_turn = ((freq_cols[None, :] * peak_col[:, None]) % length).astype(jnp.float32) * unit
    rc, rs = jnp.cos(row_turn)[:, :, None], jnp.sin(row_turn)[:, :, None]
    cc, cs = jnp.cos(col_turn)[:, None, :], jnp.sin(col_turn)[:, None, :]
    shifted = plain[:, :, 0] * (rc * cc - rs * cs) - plain[:, :, 1] * (rs * cc + rc * cs)
    binned = jnp.sum(shifted.reshape(slots, half, length // 4, 4), axis=3).astype(jnp.bfloat16)
    valid = jnp.arange(slots, dtype=jnp.int32) < peak_count[0, 0]
    binned = jnp.where(valid[:, None, None], binned, jnp.zeros_like(binned)).reshape(slots, -1)
    grid_local = ctf_grid[:, 0]
    grid_count = grid_local.shape[0]
    listed = lax.axis_size("tile") * slots
    part = lax.dot_general(
        lax.all_gather(binned, "tile", axis=0, tiled=True),
        grid_local,
        (((1,), (1,)), ((), ())),
        preferred_element_type=jnp.float32,
    )
    refined = lax.psum(part, "nar") * (1.0 / length)
    best = lax.pmax(jnp.max(refined, axis=1), "tile")
    return (
        top.reshape(1, 1, -1),
        mean.reshape(1, 1, -1),
        refined.reshape(1, listed, grid_count),
        best.reshape(1, listed),
    )


def fits(sizes, args):
    R, T, N = sizes
    _, orients, _, rows, length = args[0].shape
    half, slots, defoci = args[3].shape[3], args[6].shape[0], args[9].shape[0]
    return (
        rows % PACK == 0
        and orients * rows // PACK % 2 == 0
        and T <= 8
        and R == 4
        and T * rows == half
        and N * half == length
        and length % LANES == 0
        and length % (N * R * PACK) == 0
        and defoci == SUBL
        and defoci % R == 0
        and T * slots <= LANES
        and length // 4 <= LANES
        and args[9].shape[2] == half * (length // 4)
        and args[9].shape[2] % (R * length) == 0
    )


def solution(mesh):
    sizes = tuple(mesh.shape[axis] for axis in ("rot", "tile", "nar"))

    def body(*args):
        return fused(sizes, args) if fits(sizes, args) else shards(*args)

    return jax.shard_map(
        body,
        mesh=mesh,
        in_specs=(
            P(None, "rot", "nar", "tile", None),
            P(None, "rot", "nar", "tile", None),
            P(None, "nar", "tile", None),
            P(None, "tile", "nar", None, None),
            P("tile", "nar", None, None),
            P("rot", "tile"),
            P(("rot", "tile")),
            P(("rot", "tile")),
            P(("rot", "tile")),
            P("tile", "nar", None),
        ),
        out_specs=(
            P("tile", "nar", None),
            P("tile", "nar", None),
            P("rot", None, "tile"),
            P("rot", None),
        ),
        check_vma=False,
    )
```
